512 devices in a mesh: mp: 64 (over y, z), narrow: 8 (over x, core).
Axes of the slice: x: 4, y: 4, z: 16, core: 2. Of those that a mesh axis runs over, the one named last changes fastest.
Arguments:
- inputs: bfloat16 [512, 8192], P('mp', 'narrow'), may hold values from -36 to 36, as said below
- out_grad: bfloat16 [512, 8192], P('mp', 'narrow'), may hold values from -36 to 36, as said below
- w_in: bfloat16 [8192, 32768], P('narrow', 'mp'), may hold values from -0.0625 to 0.0625
- w_out: bfloat16 [32768, 8192], P('mp', 'narrow'), may hold values from -0.03125 to 0.03125
- row_in: float32 [8192], P('narrow'), may hold values from 0.1 to 40, as said below
- col_in: float32 [32768], P('mp'), may hold values from 0.1 to 40, as said below
- row_out: float32 [32768], P('mp'), may hold values from 0.1 to 40, as said below
- col_out: float32 [8192], P('narrow'), may hold values from 0.1 to 40, as said below
Outputs:
- input_grad: bfloat16 [512, 8192], P('mp', 'narrow')
- update_in: bfloat16 [8192, 32768], P('narrow', 'mp')
- update_out: bfloat16 [32768, 8192], P('mp', 'narrow')
- row_in_new: float32 [8192], P('narrow')
- col_in_new: float32 [32768], P('mp')
- row_out_new: float32 [32768], P('mp')
- col_out_new: float32 [8192], P('narrow')
The draws below stay inside these ranges and needn't reach their ends.
Inputs may be any that keep to these rules, and one draw needn't show every extreme that they name: `inputs`: real values. `out_grad`: real values. `row_in`: positive moments. `col_in`: positive moments. `row_out`: positive moments. `col_out`: positive moments.
All inputs are finite; a program needn't handle non-finite values.
Results may differ from the reference program's by a relative error of at most 0.005.
Values may be sent and summed in bfloat16 or wider, within the bound.
A program may use at most 64 MiB of HBM per device.

```python
import math
import jax
import jax.numpy as jnp
from jax import lax

D = 8192
FF = 32768
TOKENS = 512


def scaled_field(key, low_scale, high_scale, base):
    key_rows, key_cols = jax.random.split(key, 2)
    row_scale = jnp.exp(jax.random.uniform(key_rows, (TOKENS, 1), jnp.float32, math.log(low_scale), math.log(high_scale)))
    col_scale = jnp.exp(jax.random.uniform(key_cols, (1, D), jnp.float32, math.log(low_scale), math.log(high_scale)))
    return (base * row_scale * col_scale).astype(jnp.bfloat16)


def trended(key, length, ramp):
    base = jnp.exp(jax.random.uniform(key, (length,), jnp.float32, math.log(4.0), math.log(40.0)))
    position = jnp.arange(length, dtype=jnp.float32) / float(length)
    return base * jnp.exp(-math.log(ramp) * position)


def draw_inputs(key, part):
    key = jax.random.fold_in(key, 11)
    key_base, key_scale = jax.random.split(key, 2)
    base = jnp.clip(jax.random.normal(key_base, (TOKENS, D), jnp.float32), -4.0, 4.0)
    return scaled_field(key_scale, 0.33, 3.0, base)


def draw_out_grad(key, part):
    key = jax.random.fold_in(key, 23)
    key_base, key_scale = jax.random.split(key, 2)
    base = jnp.clip(jax.random.normal(key_base, (TOKENS, D), jnp.float32), -4.0, 4.0)
    return scaled_field(key_scale, 0.33, 3.0, base)


def draw_row_in(key, part):
    key = jax.random.fold_in(key, 31)
    return trended(key, D, 10.0)


def draw_col_in(key, part):
    key = jax.random.fold_in(key, 37)
    return trended(key, FF, 10.0)


def draw_row_out(key, part):
    key = jax.random.fold_in(key, 41)
    return trended(key, FF, 10.0)


def draw_col_out(key, part):
    key = jax.random.fold_in(key, 43)
    return trended(key, D, 10.0)


def block_levels(own_key, dims, shards, least, largest):
    def one(dim, parts):
        draws = jax.random.uniform(jax.random.fold_in(jax.random.fold_in(own_key, 6), dim), (parts,), jnp.float32, least / len(shards), largest / len(shards))
        return jnp.repeat(jnp.exp(draws), dims[dim] // parts).reshape((-1,) + (1,) * (len(dims) - dim - 1))

    level = one(*shards[0])
    for cut in shards[1:]:
        level = level * one(*cut)
    return level


def bell_draw(own_key, dims, deviation, limit, cuts=(), kind=jnp.bfloat16):
    gain = block_levels(own_key, dims, cuts, -0.22, 0.18) if cuts else 1.0
    result = jax.random.normal(own_key, dims, jnp.float32) * deviation * gain
    return jnp.minimum(jnp.maximum(result, -limit), limit).astype(kind)


def setup_inputs(seed: int = 0) -> dict:
    keys = jax.random.split(jax.random.key(seed), 9)
    inputs = draw_inputs(jax.random.fold_in(keys[8], 71), 0)
    out_grad = draw_out_grad(jax.random.fold_in(keys[8], 71), 0)
    w_in = bell_draw(keys[2], (D, FF), D ** -0.5, 0.0625, ((0, 8), (1, 64)))
    w_out = bell_draw(keys[3], (FF, D), FF ** -0.5, 0.03125, ((0, 64), (1, 8)))
    row_in = draw_row_in(jax.random.fold_in(keys[8], 71), 0)
    col_in = draw_col_in(jax.random.fold_in(keys[8], 71), 0)
    row_out = draw_row_out(jax.random.fold_in(keys[8], 71), 0)
    col_out = draw_col_out(jax.random.fold_in(keys[8], 71), 0)
    return {"inputs": inputs, "out_grad": out_grad, "w_in": w_in, "w_out": w_out, "row_in": row_in, "col_in": col_in, "row_out": row_out, "col_out": col_out}


decay_rate = 0.8
epsilon = 1e-06
clip_floor = 0.01

def silu_grad(preact):
    sigma = jax.nn.sigmoid(preact)
    return sigma * (1.0 + preact * (1.0 - sigma))

def adafactor(gradient, row_old, col_old):
    square = gradient * gradient + epsilon
    row_new = decay_rate * row_old + (1.0 - decay_rate) * lax.optimization_barrier(jnp.mean(square, axis=1))
    col_new = decay_rate * col_old + (1.0 - decay_rate) * lax.optimization_barrier(jnp.mean(square, axis=0))
    step = gradient * lax.rsqrt(row_new[:, None] * col_new[None, :])
    rms_value = jnp.sqrt(jnp.mean(step * step))
    update = (step / jnp.maximum(clip_floor, rms_value)).astype(jnp.bfloat16)
    return (update, row_new, col_new)

def reference(inputs, out_grad, w_in, w_out, row_in, col_in, row_out, col_out):
    preact = jnp.dot(inputs, w_in, preferred_element_type=jnp.float32)
    activation = jax.nn.silu(preact).astype(jnp.bfloat16)
    upstream = jnp.dot(out_grad, w_out.T, preferred_element_type=jnp.float32)
    hidden_grad = (upstream * silu_grad(preact)).astype(jnp.bfloat16)
    grad_out = jnp.dot(activation.T, out_grad, preferred_element_type=jnp.float32)
    grad_in = jnp.dot(inputs.T, hidden_grad, preferred_element_type=jnp.float32)
    input_grad = jnp.dot(hidden_grad, w_in.T, preferred_element_type=jnp.float32).astype(jnp.bfloat16)
    update_in, row_in_new, col_in_new = adafactor(grad_in, row_in, col_in)
    update_out, row_out_new, col_out_new = adafactor(grad_out, row_out, col_out)
    return (input_grad, update_in, update_out, row_in_new, col_in_new, row_out_new, col_out_new)
```

```python
import functools

import jax
import jax.numpy as jnp
from jax import lax
from jax.experimental import pallas as pl
from jax.experimental.pallas import tpu as pltpu
from jax.sharding import PartitionSpec as P

D = 8192
FF = 32768
DECAY = 0.8
EPS = 1e-06
CLIP = 0.01

NY, NZ, NX = 4, 16, 4
F32, BF16 = jnp.float32, jnp.bfloat16
MESH = pl.DeviceIdType.MESH
EXACT = lax.Precision.HIGHEST


def dot(a, b, dims, precision=None):
    return lax.dot_general(
        a, b, ((dims[0], dims[1]), ((), ())), precision=precision, preferred_element_type=F32
    )


def fold_lanes(row, parts):
    return jnp.concatenate([row[:, k * 128 : (k + 1) * 128] for k in range(parts)], axis=0)


def unfold_lanes(block, start, parts):
    return jnp.concatenate([block[start + k : start + k + 1, :] for k in range(parts)], axis=1)


def lane_fold(q):
    out = q[:, 0:128]
    for k in range(1, q.shape[1] // 128):
        out = out + q[:, k * 128 : (k + 1) * 128]
    return out


def kernel(
    x_ref, dy_ref, win_ref, wout_ref, rin_ref, cin_ref, rout_ref, cout_ref,
    ig_ref, gin_ref, gout_ref, rin_new, cin_new, rout_new, cout_new, den_ref,
    ga, xs, ds, part, cx, own, sx, xr, hh,
    ys, yr, zs, zr,
    rp_in, rp_out, cs_in, cs_out,
    my, mz, nb, nn, ny, nz,
    yg_s, yg_r, zg_s, zg_r, cx_s, cx_r, xr_s, xr_r, xg_s, xg_r, cg_s, cg_r,
    yi_s, yi_r, zi_s, zi_r, my_s, my_r, mz_s, mz_r, nb_s, nb_r, nn_s, nn_r,
    ny_s, ny_r, nz_s, nz_r,
):
    mp = lax.axis_index("mp")
    nar = lax.axis_index("narrow")
    y, z = mp // NZ, lax.rem(mp, NZ)
    x, c = nar // 2, lax.rem(nar, 2)

    def at_y(d):
        return (lax.rem(y + d, NY) * NZ + z, nar)

    def at_z(d):
        return (y * NZ + lax.rem(z + d, NZ), nar)

    def at_x(d):
        return (mp, lax.rem(x + d, NX) * 2 + c)

    def at_n(d):
        return (mp, lax.rem(nar + d, 8))

    other = (mp, x * 2 + 1 - c)

    def remote(src, dst, ssem, rsem, dev):
        return pltpu.make_async_remote_copy(
            src_ref=src, dst_ref=dst, send_sem=ssem, recv_sem=rsem,
            device_id=dev, device_id_type=MESH,
        )

    barrier = pltpu.get_barrier_semaphore()

    @pl.loop(1, NZ)
    def _(d):
        pl.semaphore_signal(barrier, inc=1, device_id=at_z(d), device_id_type=MESH)

    for d in range(1, NY):
        pl.semaphore_signal(barrier, inc=1, device_id=at_y(d), device_id_type=MESH)
    for d in range(1, 8):
        pl.semaphore_signal(barrier, inc=1, device_id=at_n(d), device_id_type=MESH)

    ga[z, y] = jnp.concatenate(
        [x_ref[...].astype(F32), dy_ref[...].astype(F32)], axis=0
    ).astype(BF16)
    pl.semaphore_wait(barrier, (NZ - 1) + (NY - 1) + 7)

    def y_copy(d):
        return remote(ga.at[z, y], ga.at[z, y], yg_s.at[d], yg_r.at[d], at_y(d))

    def z_copy(way, s, k):
        row = lax.rem(z + (NZ - s if way == 0 else s), NZ)
        col = lax.rem(y + NY - k, NY)
        return remote(
            ga.at[row, col], ga.at[row, col], zg_s.at[way, s, k], zg_r.at[way, s, k],
            at_z(1 if way == 0 else NZ - 1),
        )

    def rows_of(slab):
        block = slab.astype(F32)
        return (
            block[:, 0:8, :].reshape(32, 1024).astype(BF16),
            block[:, 8:16, :].reshape(32, 1024).astype(BF16),
        )

    def work(cells):
        got = [rows_of(ga[cell]) for cell in cells]
        xb = jnp.concatenate([g[0] for g in got], axis=0)
        db = jnp.concatenate([g[1] for g in got], axis=0)
        pre = dot(xb, win_ref[...], ((1,), (0,)))
        up = dot(db, wout_ref[...], ((1,), (1,)))
        for k, cell in enumerate(cells):
            rows = pl.ds(pl.multiple_of(cell * 32, 32), 32)
            xs[rows, :] = got[k][0]
            ds[rows, :] = got[k][1]
            half = cell // 8
            inner = pl.ds(pl.multiple_of(lax.rem(cell, 8) * 32, 32), 32)
            part[half, 0, inner, :] = pre[k * 32 : (k + 1) * 32]
            part[half, 1, inner, :] = up[k * 32 : (k + 1) * 32]

    for d in range(1, NY):
        y_copy(d).start()
    for way in range(2):
        z_copy(way, 0, 0).start()
    for k in range(1, NY):
        y_copy(k).wait_recv()
        for way in range(2):
            z_copy(way, 0, k).start()
    work([z])

    @pl.loop(1, 7)
    def _(s):
        for k in range(NY):
            for way in range(2):
                z_copy(way, s - 1, k).wait_recv()
                z_copy(way, s, k).start()
        work([lax.rem(z + NZ - s, NZ), lax.rem(z + s, NZ)])

    for k in range(NY):
        for way in range(2):
            z_copy(way, 6, k).wait_recv()
            if (k < 2) == (way == 0):
                z_copy(way, 7, k).start()
    work([lax.rem(z + NZ - 7, NZ), lax.rem(z + 7, NZ)])
    for k in range(NY):
        z_copy(0 if k < 2 else 1, 7, k).wait_recv()
    work([lax.rem(z + 8, NZ)])

    core_copy = remote(part.at[1 - c], cx, cx_s, cx_r, other)
    core_copy.start()
    core_copy.wait_recv()

    def piece(i):
        rows = pl.ds(pl.multiple_of(i * 64, 64), 64)
        return part[c, :, rows, :] + cx[:, rows, :]

    def x_copy(d):
        to = lax.rem(x + d, NX)
        return remote(sx.at[to], xr.at[x], xr_s.at[d], xr_r.at[d], at_x(d))

    for d in (2, 1, 3):
        to = lax.rem(x + d, NX)
        sx[to] = piece(to).astype(BF16)
        x_copy(d).start()
    own[...] = piece(x)
    for d in (1, 3, 2):
        x_copy(d).wait_recv()
        own[...] += xr[lax.rem(x + NX - d, NX)].astype(F32)
    pre, up = own[0], own[1]
    sig = 1.0 / (1.0 + jnp.exp(-pre))
    slot = c * NX + x
    hh[0, slot] = (pre * sig).astype(BF16)
    hh[1, slot] = (up * (sig * (1.0 + pre * (1.0 - sig)))).astype(BF16)

    def g_copy(d):
        return remote(hh.at[:, slot], hh.at[:, slot], xg_s.at[d], xg_r.at[d], at_x(d))

    def c_copy(d):
        mine = c * NX + lax.rem(x + NX - d, NX)
        return remote(hh.at[:, mine], hh.at[:, mine], cg_s.at[d], cg_r.at[d], other)

    for d in (2, 1, 3):
        g_copy(d).start()
    c_copy(0).start()
    for d in (1, 3, 2):
        g_copy(d).wait_recv()
        c_copy(d).start()
    for d in (0, 1, 3, 2):
        c_copy(d).wait_recv()

    rp_out[...] = jnp.zeros_like(rp_out)
    cs_in[...] = jnp.zeros_like(cs_in)

    @pl.loop(0, 4)
    def _(j):
        cols = pl.ds(pl.multiple_of(j * 256, 256), 256)
        g = dot(hh[0].reshape(512, 512), ds[:, cols], ((0,), (0,)))
        gout_ref[:, cols] = g
        q = g * g
        cs_out[:, cols] = jnp.sum(q, axis=0, keepdims=True)
        rp_out[...] += lane_fold(q)
        g = dot(xs[:, cols], hh[1].reshape(512, 512), ((0,), (0,)))
        gin_ref[cols, :] = g
        q = g * g
        cs_in[...] += jnp.sum(q, axis=0, keepdims=True)
        rp_in[cols, :] = lane_fold(q)

    ones = jnp.ones((8, 128), F32)
    row_sums_in = dot(ones, rp_in[...], ((1,), (1,)), EXACT)[0:1]
    row_sums_out = dot(ones, rp_out[...], ((1,), (1,)), EXACT)[0:1]
    my[y] = jnp.concatenate([fold_lanes(row_sums_in, 8), fold_lanes(cs_out[...], 8)], axis=0)
    nb[nar] = jnp.concatenate([fold_lanes(cs_in[...], 4), fold_lanes(row_sums_out, 4)], axis=0)

    def my_copy(d):
        return remote(my.at[y], my.at[y], my_s.at[d], my_r.at[d], at_y(d))

    def nb_copy(d):
        return remote(nb.at[nar], nb.at[nar], nb_s.at[d], nb_r.at[d], at_n(d))

    for d in range(1, NY):
        my_copy(d).start()
    for d in range(1, 8):
        nb_copy(d).start()

    @pl.loop(0, 4)
    def _(j):
        h = hh[1, pl.ds(j * 2, 2)].reshape(128, 512)
        p = dot(h, win_ref[...], ((1,), (1,)))
        p = jnp.concatenate([p[:, 0:512].reshape(16, 8, 512), p[:, 512:1024].reshape(16, 8, 512)], axis=1)
        p = p.astype(BF16).reshape(4, 4, 16, 512)
        for k in range(NY):
            ys[k, pl.ds(j * 4, 4)] = p[:, k]

    def yi_copy(d):
        return remote(ys.at[lax.rem(y + d, NY)], yr.at[y], yi_s.at[d], yi_r.at[d], at_y(d))

    for d in (2, 1, 3):
        yi_copy(d).start()

    for d in range(1, NY):
        my_copy(d).wait_recv()
    mz[z] = (my[0] + my[1]) + (my[2] + my[3])

    def mz_copy(d):
        return remote(mz.at[z], mz.at[z], mz_s.at[d], mz_r.at[d], at_z(d))

    @pl.loop(1, NZ)
    def _(d):
        mz_copy(d).start()

    for d in range(1, 8):
        nb_copy(d).wait_recv()
    n_sum = nb[0]
    for k in range(1, 8):
        n_sum = n_sum + nb[k]
    cin_new[...] = DECAY * cin_ref[...] + (1.0 - DECAY) * (unfold_lanes(n_sum, 0, 4) / D + EPS)
    rout_new[...] = DECAY * rout_ref[...] + (1.0 - DECAY) * (unfold_lanes(n_sum, 4, 4) / D + EPS)

    yr[y] = ys[y]
    for d in (1, 3, 2):
        yi_copy(d).wait_recv()

    def zi_copy(d):
        to = lax.rem(z + d, NZ)
        return remote(zs.at[to], zr.at[z], zi_s.at[d], zi_r.at[d], at_z(d))

    @pl.loop(0, NZ)
    def _(k):
        t = (yr[0, k].astype(F32) + yr[1, k].astype(F32)) + (
            yr[2, k].astype(F32) + yr[3, k].astype(F32)
        )
        zs[k] = t.astype(BF16)

    @pl.loop(1, NZ)
    def _(d):
        zi_copy(d).start()

    zr[z] = zs[z]

    @pl.loop(1, NZ)
    def _(d):
        mz_copy(d).wait_recv()

    m_sum = mz[0]
    for k in range(1, NZ):
        m_sum = m_sum + mz[k]
    rin_new[...] = DECAY * rin_ref[...] + (1.0 - DECAY) * (unfold_lanes(m_sum, 0, 8) / FF + EPS)
    cout_new[...] = DECAY * cout_ref[...] + (1.0 - DECAY) * (unfold_lanes(m_sum, 8, 8) / FF + EPS)

    rp_out[...] = jnp.zeros_like(rp_out)
    inv_cin = 1.0 / cin_new[...]

    @pl.loop(0, 4)
    def _(j):
        cols = pl.ds(pl.multiple_of(j * 256, 256), 256)
        g = gout_ref[:, cols]
        rp_out[...] += lane_fold(g * g * (1.0 / cout_new[:, cols]))
        g = gin_ref[cols, :]
        rp_in[cols, :] = lane_fold(g * g * inv_cin)

    inv_rin = jnp.broadcast_to(1.0 / rin_new[...], (8, 1024))
    inv_rout = jnp.broadcast_to(1.0 / rout_new[...], (8, 512))
    n_in = dot(inv_rin, rp_in[...], ((1,), (0,)), EXACT)
    n_out = dot(inv_rout, rp_out[...], ((1,), (0,)), EXACT)
    which = lax.broadcasted_iota(jnp.int32, (8, 128), 0)
    nn[nar] = jnp.where(which < 4, n_in, n_out)

    def nn_copy(d):
        return remote(nn.at[nar], nn.at[nar], nn_s.at[d], nn_r.at[d], at_n(d))

    def ny_copy(d):
        return remote(ny.at[y], ny.at[y], ny_s.at[d], ny_r.at[d], at_y(d))

    def nz_copy(d):
        return remote(nz.at[z], nz.at[z], nz_s.at[d], nz_r.at[d], at_z(d))

    for d in range(1, 8):
        nn_copy(d).start()
    for d in range(1, 8):
        nn_copy(d).wait_recv()
    t = nn[0]
    for k in range(1, 8):
        t = t + nn[k]
    ny[y] = t
    for d in range(1, NY):
        ny_copy(d).start()
    for d in range(1, NY):
        ny_copy(d).wait_recv()
    nz[z] = (ny[0] + ny[1]) + (ny[2] + ny[3])

    @pl.loop(1, NZ)
    def _(d):
        nz_copy(d).start()

    @pl.loop(1, NZ)
    def _(d):
        zi_copy(d).wait_recv()

    t = zr[0].astype(F32)
    for k in range(1, NZ):
        t = t + zr[k].astype(F32)
    ig_ref[...] = jnp.concatenate([t[0:8], t[8:16]], axis=1).astype(BF16)

    @pl.loop(1, NZ)
    def _(d):
        nz_copy(d).wait_recv()

    t = nz[0]
    for k in range(1, NZ):
        t = t + nz[k]
    total = jnp.sum(t, axis=1, keepdims=True)
    den_ref[...] = jnp.broadcast_to(
        jnp.maximum(CLIP, jnp.sqrt(total / (float(D) * float(FF)))), (8, 128)
    )

    for d in range(1, NY):
        y_copy(d).wait_send()
        x_copy(d).wait_send()
        g_copy(d).wait_send()
        my_copy(d).wait_send()
        yi_copy(d).wait_send()
        ny_copy(d).wait_send()
    core_copy.wait_send()
    for d in range(NX):
        c_copy(d).wait_send()
    for d in range(1, 8):
        nb_copy(d).wait_send()
        nn_copy(d).wait_send()

    @pl.loop(0, 7)
    def _(s):
        for k in range(NY):
            for way in range(2):
                z_copy(way, s, k).wait_send()

    for k in range(NY):
        z_copy(0 if k < 2 else 1, 7, k).wait_send()

    @pl.loop(1, NZ)
    def _(d):
        mz_copy(d).wait_send()
        zi_copy(d).wait_send()
        nz_copy(d).wait_send()


def step(*args):
    dma = pltpu.SemaphoreType.DMA
    vmem = pltpu.VMEM
    shape = jax.ShapeDtypeStruct
    outs = (
        shape((8, 1024), BF16), shape((1024, 512), F32), shape((512, 1024), F32),
        shape((1, 1024), F32), shape((1, 512), F32), shape((1, 512), F32), shape((1, 1024), F32),
        shape((8, 128), F32),
    )
    scratch = [
        vmem((NZ, NY, 16, 1024), BF16), vmem((512, 1024), BF16), vmem((512, 1024), BF16),
        vmem((2, 2, 256, 512), F32), vmem((2, 256, 512), F32), vmem((2, 64, 512), F32),
        vmem((NX, 2, 64, 512), BF16), vmem((NX, 2, 64, 512), BF16), vmem((2, 8, 64, 512), BF16),
        vmem((NY, NZ, 16, 512), BF16), vmem((NY, NZ, 16, 512), BF16),
        vmem((NZ, 16, 512), BF16), vmem((NZ, 16, 512), BF16),
        vmem((1024, 128), F32), vmem((512, 128), F32), vmem((1, 512), F32), vmem((1, 1024), F32),
        vmem((NY, 16, 128), F32), vmem((NZ, 16, 128), F32), vmem((8, 8, 128), F32),
        vmem((8, 8, 128), F32), vmem((NY, 8, 128), F32), vmem((NZ, 8, 128), F32),
        dma((NY,)), dma((NY,)), dma((2, 8, NY)), dma((2, 8, NY)), dma, dma,
        dma((NX,)), dma((NX,)), dma((NX,)), dma((NX,)), dma((NX,)), dma((NX,)),
        dma((NY,)), dma((NY,)), dma((NZ,)), dma((NZ,)), dma((NY,)), dma((NY,)),
        dma((NZ,)), dma((NZ,)), dma((8,)), dma((8,)), dma((8,)), dma((8,)),
        dma((NY,)), dma((NY,)), dma((NZ,)), dma((NZ,)),
    ]
    return pl.pallas_call(
        kernel,
        out_shape=outs,
        in_specs=[pl.BlockSpec(memory_space=pltpu.VMEM)] * 8,
        out_specs=[pl.BlockSpec(memory_space=pltpu.VMEM)] * 8,
        scratch_shapes=scratch,
        compiler_params=pltpu.CompilerParams(
            collective_id=1, has_side_effects=True, vmem_limit_bytes=56 * 2**20
        ),
        cost_estimate=pl.CostEstimate(
            flops=2700000000, bytes_accessed=8 * 2**20, transcendentals=100000
        ),
    )(*args)


def per_device(inputs, out_grad, w_in, w_out, row_in, col_in, row_out, col_out):
    line = lambda v: v.reshape(1, -1)
    ig, gin, gout, rin, cin, rout, cout, den = step(
        inputs, out_grad, w_in, w_out, line(row_in), line(col_in), line(row_out), line(col_out)
    )
    rin, cin, rout, cout = rin[0], cin[0], rout[0], cout[0]
    update_in = (gin * lax.rsqrt(rin[:, None] * cin[None, :]) / den[0, 0]).astype(BF16)
    update_out = (gout * lax.rsqrt(rout[:, None] * cout[None, :]) / den[4, 0]).astype(BF16)
    return (ig, update_in, update_out, rin, cin, rout, cout)


def solution(mesh):
    placed = (
        P("mp", "narrow"),
        P("mp", "narrow"),
        P("narrow", "mp"),
        P("mp", "narrow"),
        P("narrow"),
        P("mp"),
        P("mp"),
        P("narrow"),
    )
    return jax.shard_map(
        per_device,
        mesh=mesh,
        in_specs=placed,
        out_specs=(
            P("mp", "narrow"),
            P("narrow", "mp"),
            P("mp", "narrow"),
            P("narrow"),
            P("mp"),
            P("mp"),
            P("narrow"),
        ),
        check_vma=False,
    )
```

```python
import functools

import jax
import jax.numpy as jnp
from jax import lax
from jax.experimental import pallas as pl
from jax.experimental.pallas import tpu as pltpu
from jax.sharding import PartitionSpec as P

D = 8192
FF = 32768
DECAY = 0.8
EPS = 1e-06
CLIP = 0.01

NY, NZ, NX = 4, 16, 4
F32, BF16 = jnp.float32, jnp.bfloat16
MESH = pl.DeviceIdType.MESH
EXACT = lax.Precision.HIGHEST
LAG = (1, 3, 5, 6, 8)


def dot(a, b, dims, precision=None):
    return lax.dot_general(
        a, b, ((dims[0], dims[1]), ((), ())), precision=precision, preferred_element_type=F32
    )


def fold_lanes(row, parts):
    return jnp.concatenate([row[:, k * 128 : (k + 1) * 128] for k in range(parts)], axis=0)


def unfold_lanes(block, start, parts):
    return jnp.concatenate([block[start + k : start + k + 1, :] for k in range(parts)], axis=1)


def lane_fold(q):
    out = q[:, 0:128]
    for k in range(1, q.shape[1] // 128):
        out = out + q[:, k * 128 : (k + 1) * 128]
    return out


def columns_of(row):
    return jnp.transpose(jnp.broadcast_to(row, (128, row.shape[1])))


def kernel(
    x_ref, dy_ref, win_hbm, wout_hbm, rin_ref, cin_ref, rout_ref, cout_ref,
    ig_ref, gin_hbm, gout_hbm, rin_new, cin_new, rout_new, cout_new, den_ref,
    win_ref, wout_ref, gin_ref, gout_ref,
    ga, xs, ds, acts, hgs, keep, give, cx, tot, sx, xr, hh,
    ys, yr, zs, zr,
    rp_in, rp_out, cs_in, cs_out,
    my, mz, ty, tz, nb, nn,
    w_sem, o_sem,
    yg_s, yg_r, zg_s, zg_r, cx_s, cx_r, xr_s, xr_r, xg_s, xg_r, cg_s, cg_r,
    yi_s, yi_r, zi_s, zi_r, my_s, my_r, mz_s, mz_r, ty_s, ty_r, tz_s, tz_r,
    nb_s, nb_r, nn_s, nn_r,
):
    mp = lax.axis_index("mp")
    nar = lax.axis_index("narrow")
    y, z = mp // NZ, lax.rem(mp, NZ)
    x, c = nar // 2, lax.rem(nar, 2)

    def at_y(d):
        return (lax.rem(y + d, NY) * NZ + z, nar)

    def at_z(d):
        return (y * NZ + lax.rem(z + d, NZ), nar)

    def at_x(d):
        return (mp, lax.rem(x + d, NX) * 2 + c)

    def at_n(d):
        return (mp, lax.rem(nar + d, 8))

    other = (mp, x * 2 + 1 - c)

    def remote(src, dst, ssem, rsem, dev):
        return pltpu.make_async_remote_copy(
            src_ref=src, dst_ref=dst, send_sem=ssem, recv_sem=rsem,
            device_id=dev, device_id_type=MESH,
        )

    barrier = pltpu.get_barrier_semaphore()
    greet = [at_y(1), at_y(2), at_y(3), at_z(1), at_z(NZ - 1), at_x(1), at_x(2), at_x(3), other]
    for dev in greet:
        pl.semaphore_signal(barrier, inc=1, device_id=dev, device_id_type=MESH)

    load_in = pltpu.make_async_copy(win_hbm, win_ref, w_sem.at[0])
    load_out = pltpu.make_async_copy(wout_hbm, wout_ref, w_sem.at[1])
    load_in.start()
    load_out.start()
    ga[z, y] = jnp.concatenate(
        [x_ref[...].astype(F32), dy_ref[...].astype(F32)], axis=0
    ).astype(BF16)
    pl.semaphore_wait(barrier, len(greet))

    def y_copy(d):
        return remote(ga.at[z, y], ga.at[z, y], yg_s.at[d], yg_r.at[d], at_y(d))

    def z_copy(way, s, k):
        row = lax.rem(z + (NZ - s if way == 0 else s), NZ)
        col = lax.rem(y + NY - k, NY)
        return remote(
            ga.at[row, col], ga.at[row, col], zg_s.at[way, s, k], zg_r.at[way, s, k],
            at_z(1 if way == 0 else NZ - 1),
        )

    def pair(s):
        first = lax.rem(z + NZ - s, NZ)
        second = lax.rem(z + lax.rem(s, 8), NZ)
        return jnp.where(c == 0, first, second), jnp.where(c == 0, second, first)

    def rows32(cell):
        return pl.ds(pl.multiple_of(cell * 32, 32), 32)

    def split16(block, width):
        block = block.astype(F32)
        return (
            block[:, 0:8, :].reshape(32, width).astype(BF16),
            block[:, 8:16, :].reshape(32, width).astype(BF16),
        )

    def cx_copy(s):
        i = s - 1
        return remote(give.at[i], cx.at[i], cx_s.at[i], cx_r.at[i], other)

    def xr_copy(s, d):
        i = s - 1
        to = lax.rem(x + d, NX)
        return remote(sx.at[i, to], xr.at[i, x], xr_s.at[i, d], xr_r.at[i, d], at_x(d))

    def xg_copy(s, d):
        ref = hh.at[pair(s)[0], x]
        return remote(ref, ref, xg_s.at[s - 1, d], xg_r.at[s - 1, d], at_x(d))

    def cg_copy(s, d):
        ref = hh.at[pair(s)[0], lax.rem(x + NX - d, NX)]
        return remote(ref, ref, cg_s.at[s - 1, d], cg_r.at[s - 1, d], other)

    def yi_copy(s, d):
        i = s - 1
        to = lax.rem(y + d, NY)
        return remote(ys.at[i, to], yr.at[i, y], yi_s.at[i, d], yi_r.at[i, d], at_y(d))

    def zi_copy(d):
        to = lax.rem(z + d, NZ)
        return remote(zs.at[to], zr.at[z], zi_s.at[d], zi_r.at[d], at_z(d))

    def project(s):
        cells = pair(s)
        got = [split16(ga[cell], 1024) for cell in cells]
        xb = jnp.concatenate([g[0] for g in got], axis=0)
        db = jnp.concatenate([g[1] for g in got], axis=0)
        pre = dot(xb, win_ref[...], ((1,), (0,)))
        up = dot(db, wout_ref[...], ((1,), (1,)))
        i = s - 1
        keep[i, 0] = pre[0:32]
        keep[i, 1] = up[0:32]
        give[i, 0] = pre[32:64]
        give[i, 1] = up[32:64]
        cx_copy(s).start()
        for g, cell in zip(got, cells):
            xs[rows32(cell), :] = g[0]
            ds[rows32(cell), :] = g[1]

    def spread(s):
        i = s - 1
        cx_copy(s).wait_recv()
        t = keep[i] + cx[i]
        t = jnp.concatenate([t[0].reshape(4, 8, 512), t[1].reshape(4, 8, 512)], axis=1)
        tot[i] = t
        sx[i] = t.astype(BF16)
        for d in (2, 1, 3):
            xr_copy(s, d).start()

    def activate(s):
        i = s - 1
        t = tot[i, x]
        for d in (1, 3, 2):
            xr_copy(s, d).wait_recv()
            t = t + xr[i, lax.rem(x + NX - d, NX)].astype(F32)
        pre, up = t[0:8], t[8:16]
        sig = 1.0 / (1.0 + jnp.exp(-pre))
        hh[pair(s)[0], x] = jnp.concatenate(
            [pre * sig, up * (sig * (1.0 + pre * (1.0 - sig)))], axis=0
        ).astype(BF16)
        for d in (2, 1, 3):
            xg_copy(s, d).start()
        cg_copy(s, 0).start()

    def hand_over(s):
        for d in (1, 3, 2):
            xg_copy(s, d).wait_recv()
            cg_copy(s, d).start()

    def back_project(s):
        for d in (0, 1, 3, 2):
            cg_copy(s, d).wait_recv()
        cells = pair(s)
        got = [split16(hh[cell], 512) for cell in cells]
        p = dot(jnp.concatenate([g[1] for g in got], axis=0), win_ref[...], ((1,), (1,)))
        p = p.reshape(2, 4, 8, 1024)
        p = jnp.concatenate([p[..., 0:512], p[..., 512:1024]], axis=2).astype(BF16)
        for k in range(NY):
            ys[s - 1, k] = p[:, k]
        for d in (2, 1, 3):
            yi_copy(s, d).start()
        for g, cell in zip(got, cells):
            acts[rows32(cell), :] = g[0]
            hgs[rows32(cell), :] = g[1]

    def deliver(s):
        i = s - 1
        yr[i, y] = ys[i, y]
        for d in (1, 3, 2):
            yi_copy(s, d).wait_recv()
        t = (yr[i, 0].astype(F32) + yr[i, 1].astype(F32)) + (
            yr[i, 2].astype(F32) + yr[i, 3].astype(F32)
        )
        for k, cell in enumerate(pair(s)):
            zs[cell] = t[k].astype(BF16)

        zi_copy(NZ - s).start()

        @pl.when(s < 8)
        def _():
            zi_copy(lax.rem(s, NZ)).start()

    for d in (2, 1, 3):
        y_copy(d).start()
    for way in range(2):
        z_copy(way, 0, 0).start()
    for k in (1, 3, 2):
        y_copy(k).wait_recv()
        for way in range(2):
            z_copy(way, 0, k).start()
    load_in.wait()
    load_out.wait()

    @pl.loop(1, 8 + LAG[3] + 1)
    def _(s):
        @pl.when(s < 7)
        def _():
            for k in (0, 1, 3, 2):
                for way in range(2):
                    z_copy(way, s - 1, k).wait_recv()
                    z_copy(way, s, k).start()

        @pl.when(s == 7)
        def _():
            for k in (0, 1, 3, 2):
                for way in range(2):
                    z_copy(way, 6, k).wait_recv()
                    if (k < 2) == (way == 0):
                        z_copy(way, 7, k).start()

        @pl.when(s == 8)
        def _():
            for k in (0, 1, 3, 2):
                z_copy(0 if k < 2 else 1, 7, k).wait_recv()

        def stage(lag, run):
            @pl.when(jnp.logical_and(s > lag, s <= 8 + lag))
            def _():
                run(s - lag)

        stage(LAG[4], deliver)
        stage(LAG[3], back_project)
        stage(LAG[2], hand_over)
        stage(LAG[1], activate)
        stage(LAG[0], spread)

        @pl.when(s <= 8)
        def _():
            project(s)

    rp_out[...] = jnp.zeros_like(rp_out)
    cs_in[...] = jnp.zeros_like(cs_in)

    @pl.loop(0, 4)
    def _(j):
        cols = pl.ds(pl.multiple_of(j * 256, 256), 256)
        g = dot(acts[...], ds[:, cols], ((0,), (0,)))
        gout_ref[:, cols] = g
        q = g * g
        cs_out[:, cols] = jnp.sum(q, axis=0, keepdims=True)
        rp_out[...] += lane_fold(q)
        g = dot(xs[:, cols], hgs[...], ((0,), (0,)))
        gin_ref[cols, :] = g
        q = g * g
        cs_in[...] += jnp.sum(q, axis=0, keepdims=True)
        rp_in[cols, :] = lane_fold(q)

    save_in = pltpu.make_async_copy(gin_ref, gin_hbm, o_sem.at[0])
    save_out = pltpu.make_async_copy(gout_ref, gout_hbm, o_sem.at[1])
    ones = jnp.ones((8, 128), F32)

    def my_copy(d):
        return remote(my.at[y], my.at[y], my_s.at[d], my_r.at[d], at_y(d))

    def mz_copy(d):
        return remote(mz.at[z], mz.at[z], mz_s.at[d], mz_r.at[d], at_z(d))

    def ty_copy(d):
        return remote(ty.at[y], ty.at[y], ty_s.at[d], ty_r.at[d], at_y(d))

    def tz_copy(d):
        return remote(tz.at[z], tz.at[z], tz_s.at[d], tz_r.at[d], at_z(d))

    def nb_copy(d):
        return remote(nb.at[nar], nb.at[nar], nb_s.at[d], nb_r.at[d], at_n(d))

    def nn_copy(d):
        return remote(nn.at[nar], nn.at[nar], nn_s.at[d], nn_r.at[d], at_n(d))

    row_sums_out = dot(ones, rp_out[...], ((1,), (1,)), EXACT)[0:1]
    nb[nar] = jnp.concatenate([fold_lanes(cs_in[...], 4), fold_lanes(row_sums_out, 4)], axis=0)
    for d in range(1, 8):
        nb_copy(d).start()
    row_sums_in = dot(ones, rp_in[...], ((1,), (1,)), EXACT)[0:1]
    my[y] = jnp.concatenate([fold_lanes(row_sums_in, 8), fold_lanes(cs_out[...], 8)], axis=0)
    for d in range(1, NY):
        my_copy(d).start()
    save_in.start()
    save_out.start()

    for s in range(8 + LAG[3] - LAG[4] + 1, 9):
        deliver(s)
    zr[z] = zs[z]

    for d in range(1, 8):
        nb_copy(d).wait_recv()
    n_sum = nb[0]
    for k in range(1, 8):
        n_sum = n_sum + nb[k]
    cin_new[...] = DECAY * cin_ref[...] + (1.0 - DECAY) * (unfold_lanes(n_sum, 0, 4) / D + EPS)
    rout_new[...] = DECAY * rout_ref[...] + (1.0 - DECAY) * (unfold_lanes(n_sum, 4, 4) / D + EPS)

    inv_cin = 1.0 / cin_new[...]
    rp_out[...] = columns_of(1.0 / rout_new[...])

    @pl.loop(0, 4)
    def _(j):
        cols = pl.ds(pl.multiple_of(j * 256, 256), 256)
        g = gout_ref[:, cols]
        q = g * g
        w = rp_out[...]
        q = jnp.concatenate([q[:, 0:128] * w, q[:, 128:256] * w], axis=1)
        cs_out[:, cols] = jnp.sum(q, axis=0, keepdims=True)
        g = gin_ref[cols, :]
        rp_in[cols, :] = lane_fold(g * g * inv_cin)

    t_in = dot(ones, rp_in[...], ((1,), (1,)), EXACT)[0:1]
    ty[y] = jnp.concatenate([fold_lanes(t_in, 8), fold_lanes(cs_out[...], 8)], axis=0)
    for d in range(1, NY):
        ty_copy(d).start()

    for d in range(1, NY):
        my_copy(d).wait_recv()
    mz[z] = (my[0] + my[1]) + (my[2] + my[3])

    @pl.loop(1, NZ)
    def _(d):
        mz_copy(d).start()

    for d in range(1, NY):
        ty_copy(d).wait_recv()
    tz[z] = ((ty[0] + ty[1]) + (ty[2] + ty[3])).astype(BF16)

    @pl.loop(1, NZ)
    def _(d):
        tz_copy(d).start()

    @pl.loop(1, NZ)
    def _(d):
        zi_copy(d).wait_recv()

    t = zr[0].astype(F32)
    for k in range(1, NZ):
        t = t + zr[k].astype(F32)
    ig_ref[...] = jnp.concatenate([t[0:8], t[8:16]], axis=1).astype(BF16)

    @pl.loop(1, NZ)
    def _(d):
        mz_copy(d).wait_recv()

    m_sum = mz[0]
    for k in range(1, NZ):
        m_sum = m_sum + mz[k]
    r_new = DECAY * rin_ref[...] + (1.0 - DECAY) * (unfold_lanes(m_sum, 0, 8) / FF + EPS)
    c_new = DECAY * cout_ref[...] + (1.0 - DECAY) * (unfold_lanes(m_sum, 8, 8) / FF + EPS)
    rin_new[...] = r_new
    cout_new[...] = c_new
    inv_r, inv_c = fold_lanes(1.0 / r_new, 8), fold_lanes(1.0 / c_new, 8)

    @pl.loop(1, NZ)
    def _(d):
        tz_copy(d).wait_recv()

    t = tz[0].astype(F32)
    for k in range(1, NZ):
        t = t + tz[k].astype(F32)
    n_in = jnp.sum(t[0:8] * inv_r, axis=0, keepdims=True)
    n_out = jnp.sum(t[8:16] * inv_c, axis=0, keepdims=True)
    which = lax.broadcasted_iota(jnp.int32, (8, 128), 0)
    nn[nar] = jnp.where(which < 4, n_in, n_out)
    for d in range(1, 8):
        nn_copy(d).start()
    for d in range(1, 8):
        nn_copy(d).wait_recv()
    t = nn[0]
    for k in range(1, 8):
        t = t + nn[k]
    total = jnp.sum(t, axis=1, keepdims=True)
    den_ref[...] = jnp.broadcast_to(
        jnp.maximum(CLIP, jnp.sqrt(total / (float(D) * float(FF)))), (8, 128)
    )

    save_in.wait()
    save_out.wait()
    for d in range(1, NY):
        y_copy(d).wait_send()
        my_copy(d).wait_send()
        ty_copy(d).wait_send()

    @pl.loop(1, 9)
    def _(s):
        cx_copy(s).wait_send()
        cg_copy(s, 0).wait_send()
        for d in range(1, NX):
            xr_copy(s, d).wait_send()
            xg_copy(s, d).wait_send()
            cg_copy(s, d).wait_send()
            yi_copy(s, d).wait_send()

    for d in range(1, 8):
        nb_copy(d).wait_send()
        nn_copy(d).wait_send()

    @pl.loop(0, 7)
    def _(s):
        for k in range(NY):
            for way in range(2):
                z_copy(way, s, k).wait_send()

    for k in range(NY):
        z_copy(0 if k < 2 else 1, 7, k).wait_send()

    @pl.loop(1, NZ)
    def _(d):
        mz_copy(d).wait_send()
        tz_copy(d).wait_send()
        zi_copy(d).wait_send()


VMEM_SPEC = pl.BlockSpec(memory_space=pltpu.VMEM)
ANY_SPEC = pl.BlockSpec(memory_space=pl.ANY)


def step(*args):
    dma = pltpu.SemaphoreType.DMA
    vmem = pltpu.VMEM
    shape = jax.ShapeDtypeStruct
    outs = (
        shape((8, 1024), BF16), shape((1024, 512), F32), shape((512, 1024), F32),
        shape((1, 1024), F32), shape((1, 512), F32), shape((1, 512), F32), shape((1, 1024), F32),
        shape((8, 128), F32),
    )
    scratch = [
        vmem((1024, 512), BF16), vmem((512, 1024), BF16),
        vmem((1024, 512), F32), vmem((512, 1024), F32),
        vmem((NZ, NY, 16, 1024), BF16), vmem((512, 1024), BF16), vmem((512, 1024), BF16),
        vmem((512, 512), BF16), vmem((512, 512), BF16),
        vmem((8, 2, 32, 512), F32), vmem((8, 2, 32, 512), F32), vmem((8, 2, 32, 512), F32),
        vmem((8, NX, 16, 512), F32), vmem((8, NX, 16, 512), BF16), vmem((8, NX, 16, 512), BF16),
        vmem((NZ, NX, 16, 512), BF16),
        vmem((8, NY, 2, 16, 512), BF16), vmem((8, NY, 2, 16, 512), BF16),
        vmem((NZ, 16, 512), BF16), vmem((NZ, 16, 512), BF16),
        vmem((1024, 128), F32), vmem((512, 128), F32), vmem((1, 512), F32), vmem((1, 1024), F32),
        vmem((NY, 16, 128), F32), vmem((NZ, 16, 128), F32),
        vmem((NY, 16, 128), F32), vmem((NZ, 16, 128), BF16),
        vmem((8, 8, 128), F32), vmem((8, 8, 128), F32),
        dma((2,)), dma((2,)),
        dma((NY,)), dma((NY,)), dma((2, 8, NY)), dma((2, 8, NY)), dma((8,)), dma((8,)),
        dma((8, NX)), dma((8, NX)), dma((8, NX)), dma((8, NX)), dma((8, NX)), dma((8, NX)),
        dma((8, NY)), dma((8, NY)), dma((NZ,)), dma((NZ,)),
        dma((NY,)), dma((NY,)), dma((NZ,)), dma((NZ,)),
        dma((NY,)), dma((NY,)), dma((NZ,)), dma((NZ,)),
        dma((8,)), dma((8,)), dma((8,)), dma((8,)),
    ]
    return pl.pallas_call(
        kernel,
        out_shape=outs,
        in_specs=[VMEM_SPEC, VMEM_SPEC, ANY_SPEC, ANY_SPEC] + [VMEM_SPEC] * 4,
        out_specs=[VMEM_SPEC, ANY_SPEC, ANY_SPEC] + [VMEM_SPEC] * 5,
        scratch_shapes=scratch,
        compiler_params=pltpu.CompilerParams(
            collective_id=1, has_side_effects=True, vmem_limit_bytes=56 * 2**20
        ),
        cost_estimate=pl.CostEstimate(
            flops=2700000000, bytes_accessed=8 * 2**20, transcendentals=100000
        ),
    )(*args)


STEPS = 4


def scale_kernel(
    ig_ref, gin_ref, gout_ref, rin_ref, cin_ref, rout_ref, cout_ref, den_ref,
    ig_out, uin_ref, uout_ref, rin_out, cin_out, rout_out, cout_out,
):
    j = pl.program_id(0)

    @pl.when(j == 0)
    def _():
        ig_out[...] = ig_ref[...]
        rin_out[...] = fold_lanes(rin_ref[...], 8)
        cin_out[...] = fold_lanes(cin_ref[...], 4)
        rout_out[...] = fold_lanes(rout_ref[...], 4)
        cout_out[...] = fold_lanes(cout_ref[...], 8)

    def update(g_ref, row, col_ref, den, u_ref):
        r = columns_of(row)
        for k in range(g_ref.shape[1] // 128):
            lanes = slice(k * 128, (k + 1) * 128)
            u_ref[:, lanes] = (
                g_ref[:, lanes] * lax.rsqrt(r * col_ref[:, lanes]) / den
            ).astype(BF16)

    many, few = 1024 // STEPS, 512 // STEPS
    update(
        gin_ref, rin_ref[:, pl.ds(pl.multiple_of(j * many, many), many)], cin_ref,
        den_ref[0:1, :], uin_ref,
    )
    update(
        gout_ref, rout_ref[:, pl.ds(pl.multiple_of(j * few, few), few)], cout_ref,
        den_ref[4:5, :], uout_ref,
    )


def scale(*args):
    shape = jax.ShapeDtypeStruct
    whole = lambda *dims: pl.BlockSpec(dims, lambda j: (0, 0))
    big = lambda *dims: pl.BlockSpec(dims, lambda j: (j, 0))
    return pl.pallas_call(
        scale_kernel,
        grid=(STEPS,),
        in_specs=[
            whole(8, 1024), big(1024 // STEPS, 512), big(512 // STEPS, 1024),
            whole(1, 1024), whole(1, 512), whole(1, 512), whole(1, 1024), whole(8, 128),
        ],
        out_specs=[
            whole(8, 1024), big(1024 // STEPS, 512), big(512 // STEPS, 1024),
            whole(8, 128), whole(4, 128), whole(4, 128), whole(8, 128),
        ],
        out_shape=(
            shape((8, 1024), BF16), shape((1024, 512), BF16), shape((512, 1024), BF16),
            shape((8, 128), F32), shape((4, 128), F32), shape((4, 128), F32), shape((8, 128), F32),
        ),
        compiler_params=pltpu.CompilerParams(vmem_limit_bytes=56 * 2**20),
    )(*args)


def per_device(inputs, out_grad, w_in, w_out, row_in, col_in, row_out, col_out):
    line = lambda v: v.reshape(1, -1)
    whole = step(
        inputs, out_grad, w_in, w_out, line(row_in), line(col_in), line(row_out), line(col_out)
    )
    ig, update_in, update_out, rin, cin, rout, cout = scale(*whole)
    return (
        ig, update_in, update_out,
        rin.reshape(-1), cin.reshape(-1), rout.reshape(-1), cout.reshape(-1),
    )


def solution(mesh):
    placed = (
        P("mp", "narrow"),
        P("mp", "narrow"),
        P("narrow", "mp"),
        P("mp", "narrow"),
        P("narrow"),
        P("mp"),
        P("mp"),
        P("narrow"),
    )
    return jax.shard_map(
        per_device,
        mesh=mesh,
        in_specs=placed,
        out_specs=(
            P("mp", "narrow"),
            P("narrow", "mp"),
            P("mp", "narrow"),
            P("narrow"),
            P("mp"),
            P("mp"),
            P("narrow"),
        ),
        check_vma=False,
    )
```

```python
import functools

import jax
import jax.numpy as jnp
from jax import lax
from jax.experimental import pallas as pl
from jax.experimental.pallas import tpu as pltpu
from jax.sharding import PartitionSpec as P

D = 8192
FF = 32768
DECAY = 0.8
EPS = 1e-06
CLIP = 0.01

NY, NZ, NX = 4, 16, 4
F32, BF16 = jnp.float32, jnp.bfloat16
MESH = pl.DeviceIdType.MESH
EXACT = lax.Precision.HIGHEST
LAG = (1, 3, 5, 7)
FAR_FIRST = (8, 7, 9, 6, 10, 5, 11, 4, 12, 3, 13, 2, 14, 1, 15)


def dot(a, b, dims, precision=None):
    return lax.dot_general(
        a, b, ((dims[0], dims[1]), ((), ())), precision=precision, preferred_element_type=F32
    )


def fold_lanes(row, parts):
    return jnp.concatenate([row[:, k * 128 : (k + 1) * 128] for k in range(parts)], axis=0)


def unfold_lanes(block, start, parts):
    return jnp.concatenate([block[start + k : start + k + 1, :] for k in range(parts)], axis=1)


def lane_fold(q):
    out = q[:, 0:128]
    for k in range(1, q.shape[1] // 128):
        out = out + q[:, k * 128 : (k + 1) * 128]
    return out


def columns_of(row):
    return jnp.transpose(jnp.broadcast_to(row, (128, row.shape[1])))


def kernel(
    x_hbm, dy_hbm, win_hbm, wout_hbm, rin_hbm, cin_hbm, rout_hbm, cout_hbm,
    ig_hbm, gin_hbm, gout_hbm, vec_hbm,
    x_ref, dy_ref, win_ref, wout_ref, rin_ref, cin_ref, rout_ref, cout_ref,
    ig_ref, gin_ref, gout_ref, vec_ref,
    g1, g2, xs, ds, acts, hgs, keep, give, cx, tot, sx, xr, hh,
    ys, yr, zs, zr,
    rp_in, rp_out, cs_in, cs_out,
    my, mz, ty, tz, nb, nn,
    w_sem, o_sem,
    yg_s, yg_r, zg_s, zg_r, y2_s, y2_r, z2_s, z2_r, cx_s, cx_r, xr_s, xr_r, xg_s, xg_r,
    yi_s, yi_r, zi_s, zi_r, my_s, my_r, mz_s, mz_r, ty_s, ty_r, tz_s, tz_r,
    nb_s, nb_r, nn_s, nn_r,
):
    mp = lax.axis_index("mp")
    nar = lax.axis_index("narrow")
    y, z = mp // NZ, lax.rem(mp, NZ)
    x, c = nar // 2, lax.rem(nar, 2)

    def at_y(d):
        return (lax.rem(y + d, NY) * NZ + z, nar)

    def at_z(d):
        return (y * NZ + lax.rem(z + d, NZ), nar)

    def at_x(d):
        return (mp, lax.rem(x + d, NX) * 2 + c)

    def at_n(d):
        return (mp, lax.rem(nar + d, 8))

    other = (mp, x * 2 + 1 - c)

    def remote(src, dst, ssem, rsem, dev):
        return pltpu.make_async_remote_copy(
            src_ref=src, dst_ref=dst, send_sem=ssem, recv_sem=rsem,
            device_id=dev, device_id_type=MESH,
        )

    barrier = pltpu.get_barrier_semaphore()
    greet = [at_y(1), at_y(2), at_y(3), at_z(1), at_z(NZ - 1), at_x(1), at_x(2), at_x(3), other]
    for dev in greet:
        pl.semaphore_signal(barrier, inc=1, device_id=dev, device_id_type=MESH)

    loads = [
        pltpu.make_async_copy(src, dst, w_sem.at[k])
        for k, (src, dst) in enumerate((
            (x_hbm, x_ref), (dy_hbm, dy_ref), (win_hbm, win_ref), (wout_hbm, wout_ref),
            (rin_hbm, rin_ref), (cin_hbm, cin_ref), (rout_hbm, rout_ref), (cout_hbm, cout_ref),
        ))
    ]
    for load in loads:
        load.start()
    loads[0].wait()
    loads[1].wait()
    mine = jnp.concatenate([x_ref[...].astype(F32), dy_ref[...].astype(F32)], axis=0).astype(BF16)
    g1[z, y] = mine[:, 0:512]
    g2[z, y] = mine[:, 512:1024]
    vec_ref[...] = jnp.zeros_like(vec_ref)
    pl.semaphore_wait(barrier, len(greet))

    def y_copy(d):
        return remote(g1.at[z, y], g1.at[z, y], yg_s.at[d], yg_r.at[d], at_y(d))

    def z_copy(way, s, k):
        row = lax.rem(z + (NZ - s if way == 0 else s), NZ)
        col = lax.rem(y + NY - k, NY)
        return remote(
            g1.at[row, col], g1.at[row, col], zg_s.at[way, s, k], zg_r.at[way, s, k],
            at_z(1 if way == 0 else NZ - 1),
        )

    def z2_copy(way, s):
        row = lax.rem(z + (NZ - s if way == 0 else s), NZ)
        ref = g2.at[row, y]
        return remote(ref, ref, z2_s.at[way, s], z2_r.at[way, s], at_z(1 if way == 0 else NZ - 1))

    def y2_copy(way, s, d):
        row = lax.rem(z + (NZ - s if way == 0 else s), NZ)
        ref = g2.at[row, y]
        return remote(ref, ref, y2_s.at[way, s, d], y2_r.at[way, s, d], at_y(d))

    def pair(s):
        first = lax.rem(z + NZ - s, NZ)
        second = lax.rem(z + lax.rem(s, 8), NZ)
        return jnp.where(c == 0, first, second), jnp.where(c == 0, second, first)

    def rows32(cell):
        return pl.ds(pl.multiple_of(cell * 32, 32), 32)

    def split16(block, width):
        block = block.astype(F32)
        return (
            block[:, 0:8, :].reshape(32, width).astype(BF16),
            block[:, 8:16, :].reshape(32, width).astype(BF16),
        )

    def cx_copy(s):
        i = s - 1
        return remote(give.at[i], cx.at[i], cx_s.at[i], cx_r.at[i], other)

    def xr_copy(s, d):
        i = s - 1
        to = lax.rem(x + d, NX)
        return remote(sx.at[i, to], xr.at[i, x], xr_s.at[i, d], xr_r.at[i, d], at_x(d))

    def xg_copy(s, k):
        d, flip = k // 2, k % 2
        ref = hh.at[pair(s)[0], x]
        core = 1 - c if flip else c
        dev = (mp, lax.rem(x + d, NX) * 2 + core)
        return remote(ref, ref, xg_s.at[s - 1, k], xg_r.at[s - 1, k], dev)

    def yi_copy(s, d):
        i = s - 1
        to = lax.rem(y + d, NY)
        return remote(ys.at[i, to], yr.at[i, y], yi_s.at[i, d], yi_r.at[i, d], at_y(d))

    def zi_copy(d):
        to = lax.rem(z + d, NZ)
        return remote(zs.at[to], zr.at[z], zi_s.at[d], zi_r.at[d], at_z(d))

    def project(s):
        cells = pair(s)
        got = []
        for cell in cells:
            low, high = split16(g1[cell], 512), split16(g2[cell], 512)
            got.append([jnp.concatenate([a, b], axis=1) for a, b in zip(low, high)])
        xb = jnp.concatenate([g[0] for g in got], axis=0)
        db = jnp.concatenate([g[1] for g in got], axis=0)
        pre = dot(xb, win_ref[...], ((1,), (0,)))
        up = dot(db, wout_ref[...], ((1,), (1,)))
        i = s - 1
        keep[i, 0] = pre[0:32]
        keep[i, 1] = up[0:32]
        give[i, 0] = pre[32:64]
        give[i, 1] = up[32:64]
        cx_copy(s).start()
        for g, cell in zip(got, cells):
            xs[rows32(cell), :] = g[0]
            ds[rows32(cell), :] = g[1]

    def spread(s):
        i = s - 1
        cx_copy(s).wait_recv()
        t = keep[i] + cx[i]
        t = jnp.concatenate([t[0].reshape(4, 8, 512), t[1].reshape(4, 8, 512)], axis=1)
        tot[i] = t
        sx[i] = t.astype(BF16)
        for d in (2, 1, 3):
            xr_copy(s, d).start()

    def activate(s):
        i = s - 1
        t = tot[i, x]
        for d in (1, 3, 2):
            xr_copy(s, d).wait_recv()
            t = t + xr[i, lax.rem(x + NX - d, NX)].astype(F32)
        pre, up = t[0:8], t[8:16]
        sig = 1.0 / (1.0 + jnp.exp(-pre))
        hh[pair(s)[0], x] = jnp.concatenate(
            [pre * sig, up * (sig * (1.0 + pre * (1.0 - sig)))], axis=0
        ).astype(BF16)
        for k in (4, 5, 2, 6, 3, 7, 1):
            xg_copy(s, k).start()

    def back_project(s):
        for k in range(1, 8):
            xg_copy(s, k).wait_recv()
        cells = pair(s)
        got = [split16(hh[cell], 512) for cell in cells]
        p = dot(jnp.concatenate([g[1] for g in got], axis=0), win_ref[...], ((1,), (1,)))
        p = p.reshape(2, 4, 8, 1024)
        p = jnp.concatenate([p[..., 0:512], p[..., 512:1024]], axis=2).astype(BF16)
        for k in range(NY):
            ys[s - 1, k] = p[:, k]
        for d in (2, 1, 3):
            yi_copy(s, d).start()
        for g, cell in zip(got, cells):
            acts[rows32(cell), :] = g[0]
            hgs[rows32(cell), :] = g[1]

    def deliver(s):
        i = s - 1
        yr[i, y] = ys[i, y]
        for d in (1, 3, 2):
            yi_copy(s, d).wait_recv()
        t = (yr[i, 0].astype(F32) + yr[i, 1].astype(F32)) + (
            yr[i, 2].astype(F32) + yr[i, 3].astype(F32)
        )
        for k, cell in enumerate(pair(s)):
            zs[cell] = t[k].astype(BF16)

        zi_copy(NZ - s).start()

        @pl.when(s < 8)
        def _():
            zi_copy(lax.rem(s, NZ)).start()

    for d in (2, 1, 3):
        y_copy(d).start()
    for way in range(2):
        z2_copy(way, 0).start()
        z_copy(way, 0, 0).start()
    for d in (2, 1, 3):
        y2_copy(0, 0, d).start()
    for k in (1, 3, 2):
        y_copy(k).wait_recv()
        for way in range(2):
            z_copy(way, 0, k).start()
    for way in range(2):
        z2_copy(way, 0).wait_recv()
        z2_copy(way, 1).start()
        for d in (2, 1, 3):
            y2_copy(way, 1, d).start()
    for load in loads[2:]:
        load.wait()

    @pl.loop(1, 8 + LAG[2] + 1)
    def _(s):
        @pl.when(s < 7)
        def _():
            for way in range(2):
                z2_copy(way, s).wait_recv()
                if way == 0:
                    z2_copy(0, s + 1).start()
                else:

                    @pl.when(s < 6)
                    def _():
                        z2_copy(1, s + 1).start()

                for d in (2, 1, 3):
                    y2_copy(way, s + 1, d).start()
            for k in (0, 1, 3, 2):
                for way in range(2):
                    z_copy(way, s - 1, k).wait_recv()
                    z_copy(way, s, k).start()

        @pl.when(s == 7)
        def _():
            z2_copy(0, 7).wait_recv()
            for d in (2, 1, 3):
                y2_copy(0, 8, d).start()
            for k in (0, 1, 3, 2):
                for way in range(2):
                    z_copy(way, 6, k).wait_recv()
                    if (k < 2) == (way == 0):
                        z_copy(way, 7, k).start()

        @pl.when(s < 8)
        def _():
            for way in range(2):
                for d in (1, 3, 2):
                    y2_copy(way, s, d).wait_recv()

        @pl.when(s == 8)
        def _():
            for k in (0, 1, 3, 2):
                z_copy(0 if k < 2 else 1, 7, k).wait_recv()
            for d in (1, 3, 2):
                y2_copy(0, 0, d).wait_recv()
                y2_copy(0, 8, d).wait_recv()

        def stage(lag, run):
            @pl.when(jnp.logical_and(s > lag, s <= 8 + lag))
            def _():
                run(s - lag)

        stage(LAG[0], spread)
        stage(LAG[1], activate)

        @pl.when(s <= 8)
        def _():
            project(s)

        stage(LAG[2], back_project)
        stage(LAG[3], deliver)

    rp_out[...] = jnp.zeros_like(rp_out)
    cs_in[...] = jnp.zeros_like(cs_in)

    @pl.loop(0, 4)
    def _(j):
        cols = pl.ds(pl.multiple_of(j * 256, 256), 256)
        g = dot(acts[...], ds[:, cols], ((0,), (0,)))
        gout_ref[:, cols] = g
        q = g * g
        cs_out[:, cols] = jnp.sum(q, axis=0, keepdims=True)
        rp_out[...] += lane_fold(q)
        g = dot(xs[:, cols], hgs[...], ((0,), (0,)))
        gin_ref[cols, :] = g
        q = g * g
        cs_in[...] += jnp.sum(q, axis=0, keepdims=True)
        rp_in[cols, :] = lane_fold(q)

    save_in = pltpu.make_async_copy(gin_ref, gin_hbm, o_sem.at[0])
    save_out = pltpu.make_async_copy(gout_ref, gout_hbm, o_sem.at[1])
    save_ig = pltpu.make_async_copy(ig_ref, ig_hbm, o_sem.at[2])
    save_vec = pltpu.make_async_copy(vec_ref, vec_hbm, o_sem.at[3])
    ones = jnp.ones((8, 128), F32)

    def my_copy(d):
        return remote(my.at[y], my.at[y], my_s.at[d], my_r.at[d], at_y(d))

    def mz_copy(d):
        return remote(mz.at[z], mz.at[z], mz_s.at[d], mz_r.at[d], at_z(d))

    def ty_copy(d):
        return remote(ty.at[y], ty.at[y], ty_s.at[d], ty_r.at[d], at_y(d))

    def tz_copy(d):
        return remote(tz.at[z], tz.at[z], tz_s.at[d], tz_r.at[d], at_z(d))

    def nb_copy(d):
        return remote(nb.at[nar], nb.at[nar], nb_s.at[d], nb_r.at[d], at_n(d))

    def nn_copy(d):
        return remote(nn.at[nar], nn.at[nar], nn_s.at[d], nn_r.at[d], at_n(d))

    row_sums_out = dot(ones, rp_out[...], ((1,), (1,)), EXACT)[0:1]
    nb[nar] = jnp.concatenate([fold_lanes(cs_in[...], 4), fold_lanes(row_sums_out, 4)], axis=0)
    for d in range(1, 8):
        nb_copy(d).start()
    row_sums_in = dot(ones, rp_in[...], ((1,), (1,)), EXACT)[0:1]
    my[y] = jnp.concatenate([fold_lanes(row_sums_in, 8), fold_lanes(cs_out[...], 8)], axis=0)
    for d in range(1, NY):
        my_copy(d).start()

    for s in range(8 + LAG[2] - LAG[3] + 1, 9):
        deliver(s)
    zr[z] = zs[z]

    for d in range(1, 8):
        nb_copy(d).wait_recv()
    n_sum = nb[0]
    for k in range(1, 8):
        n_sum = n_sum + nb[k]
    cin_new = DECAY * cin_ref[...] + (1.0 - DECAY) * (unfold_lanes(n_sum, 0, 4) / D + EPS)
    rout_new = DECAY * rout_ref[...] + (1.0 - DECAY) * (unfold_lanes(n_sum, 4, 4) / D + EPS)
    vec_ref[2:3, 0:512] = cin_new
    vec_ref[2:3, 512:1024] = rout_new

    inv_cin = 1.0 / cin_new
    rp_out[...] = columns_of(1.0 / rout_new)

    @pl.loop(0, 4)
    def _(j):
        cols = pl.ds(pl.multiple_of(j * 256, 256), 256)
        g = gout_ref[:, cols]
        q = g * g
        w = rp_out[...]
        q = jnp.concatenate([q[:, 0:128] * w, q[:, 128:256] * w], axis=1)
        cs_out[:, cols] = jnp.sum(q, axis=0, keepdims=True)
        g = gin_ref[cols, :]
        rp_in[cols, :] = lane_fold(g * g * inv_cin)

    t_in = dot(ones, rp_in[...], ((1,), (1,)), EXACT)[0:1]
    ty[y] = jnp.concatenate([fold_lanes(t_in, 8), fold_lanes(cs_out[...], 8)], axis=0)
    for d in range(1, NY):
        ty_copy(d).start()

    for d in range(1, NY):
        my_copy(d).wait_recv()
    mz[z] = ((my[0] + my[1]) + (my[2] + my[3])).astype(BF16)

    for d in FAR_FIRST:
        mz_copy(d).start()

    for d in range(1, NY):
        ty_copy(d).wait_recv()
    tz[z] = ((ty[0] + ty[1]) + (ty[2] + ty[3])).astype(BF16)

    for d in FAR_FIRST:
        tz_copy(d).start()

    @pl.loop(1, NZ)
    def _(d):
        zi_copy(d).wait_recv()

    t = zr[0].astype(F32)
    for k in range(1, NZ):
        t = t + zr[k].astype(F32)
    ig_ref[...] = jnp.concatenate([t[0:8], t[8:16]], axis=1).astype(BF16)
    save_ig.start()

    @pl.loop(1, NZ)
    def _(d):
        mz_copy(d).wait_recv()

    m_sum = mz[0].astype(F32)
    for k in range(1, NZ):
        m_sum = m_sum + mz[k].astype(F32)
    r_new = DECAY * rin_ref[...] + (1.0 - DECAY) * (unfold_lanes(m_sum, 0, 8) / FF + EPS)
    c_new = DECAY * cout_ref[...] + (1.0 - DECAY) * (unfold_lanes(m_sum, 8, 8) / FF + EPS)
    vec_ref[0:1, :] = r_new
    vec_ref[1:2, :] = c_new
    inv_r, inv_c = fold_lanes(1.0 / r_new, 8), fold_lanes(1.0 / c_new, 8)

    rp_in[...] = columns_of(r_new)
    rp_out[...] = columns_of(rout_new)

    @pl.loop(0, 8)
    def _(j):
        rows = pl.ds(pl.multiple_of(j * 128, 128), 128)
        r = rp_in[rows, :]
        for k in range(4):
            lanes = slice(k * 128, (k + 1) * 128)
            gin_ref[rows, lanes] = gin_ref[rows, lanes] * lax.rsqrt(r * vec_ref[2:3, lanes])
        rows = pl.ds(pl.multiple_of(j * 64, 64), 64)
        r = rp_out[rows, :]
        for k in range(8):
            lanes = slice(k * 128, (k + 1) * 128)
            gout_ref[rows, lanes] = gout_ref[rows, lanes] * lax.rsqrt(r * vec_ref[1:2, lanes])

    save_in.start()
    save_out.start()

    @pl.loop(1, NZ)
    def _(d):
        tz_copy(d).wait_recv()

    t = tz[0].astype(F32)
    for k in range(1, NZ):
        t = t + tz[k].astype(F32)
    n_in = jnp.sum(t[0:8] * inv_r, axis=0, keepdims=True)
    n_out = jnp.sum(t[8:16] * inv_c, axis=0, keepdims=True)
    which = lax.broadcasted_iota(jnp.int32, (8, 128), 0)
    nn[nar] = jnp.where(which < 4, n_in, n_out)
    for d in range(1, 8):
        nn_copy(d).start()
    for d in range(1, 8):
        nn_copy(d).wait_recv()
    t = nn[0]
    for k in range(1, 8):
        t = t + nn[k]
    total = jnp.sum(t, axis=1, keepdims=True)
    inv = 1.0 / jnp.maximum(CLIP, jnp.sqrt(total / (float(D) * float(FF))))
    vec_ref[3:4, 0:512] = jnp.broadcast_to(inv[0:1], (1, 512))
    vec_ref[3:4, 512:1024] = jnp.broadcast_to(inv[4:5], (1, 512))
    save_vec.start()

    for d in range(1, NY):
        y_copy(d).wait_send()
        my_copy(d).wait_send()
        ty_copy(d).wait_send()

    @pl.loop(1, 9)
    def _(s):
        cx_copy(s).wait_send()
        for k in range(1, 8):
            xg_copy(s, k).wait_send()
        for d in range(1, NX):
            xr_copy(s, d).wait_send()
            yi_copy(s, d).wait_send()

    for d in range(1, 8):
        nb_copy(d).wait_send()
        nn_copy(d).wait_send()

    @pl.loop(0, 7)
    def _(s):
        for k in range(NY):
            for way in range(2):
                z_copy(way, s, k).wait_send()
        for way in range(2):
            z2_copy(way, s).wait_send()
            for d in range(1, NY):
                y2_copy(way, s + 1, d).wait_send()

    for k in range(NY):
        z_copy(0 if k < 2 else 1, 7, k).wait_send()
    z2_copy(0, 7).wait_send()
    for d in range(1, NY):
        y2_copy(0, 0, d).wait_send()
        y2_copy(0, 8, d).wait_send()

    @pl.loop(1, NZ)
    def _(d):
        mz_copy(d).wait_send()
        tz_copy(d).wait_send()
        zi_copy(d).wait_send()

    for save in (save_in, save_out, save_ig, save_vec):
        save.wait()


ANY_SPEC = pl.BlockSpec(memory_space=pl.ANY)


def step(*args):
    dma = pltpu.SemaphoreType.DMA
    vmem = pltpu.VMEM
    shape = jax.ShapeDtypeStruct
    outs = (
        shape((8, 1024), BF16), shape((1024, 512), F32), shape((512, 1024), F32),
        shape((8, 1024), F32),
    )
    scratch = [
        vmem((8, 1024), BF16), vmem((8, 1024), BF16), vmem((1024, 512), BF16), vmem((512, 1024), BF16),
        vmem((1, 1024), F32), vmem((1, 512), F32), vmem((1, 512), F32), vmem((1, 1024), F32),
        vmem((8, 1024), BF16), vmem((1024, 512), F32), vmem((512, 1024), F32), vmem((8, 1024), F32),
        vmem((NZ, NY, 16, 512), BF16), vmem((NZ, NY, 16, 512), BF16),
        vmem((512, 1024), BF16), vmem((512, 1024), BF16),
        vmem((512, 512), BF16), vmem((512, 512), BF16),
        vmem((8, 2, 32, 512), F32), vmem((8, 2, 32, 512), F32), vmem((8, 2, 32, 512), F32),
        vmem((8, NX, 16, 512), F32), vmem((8, NX, 16, 512), BF16), vmem((8, NX, 16, 512), BF16),
        vmem((NZ, NX, 16, 512), BF16),
        vmem((8, NY, 2, 16, 512), BF16), vmem((8, NY, 2, 16, 512), BF16),
        vmem((NZ, 16, 512), BF16), vmem((NZ, 16, 512), BF16),
        vmem((1024, 128), F32), vmem((512, 128), F32), vmem((1, 512), F32), vmem((1, 1024), F32),
        vmem((NY, 16, 128), F32), vmem((NZ, 16, 128), BF16),
        vmem((NY, 16, 128), F32), vmem((NZ, 16, 128), BF16),
        vmem((8, 8, 128), F32), vmem((8, 8, 128), F32),
        dma((8,)), dma((4,)),
        dma((NY,)), dma((NY,)), dma((2, 8, NY)), dma((2, 8, NY)),
        dma((2, 9, NY)), dma((2, 9, NY)), dma((2, 8)), dma((2, 8)), dma((8,)), dma((8,)),
        dma((8, NX)), dma((8, NX)), dma((8, 8)), dma((8, 8)),
        dma((8, NY)), dma((8, NY)), dma((NZ,)), dma((NZ,)),
        dma((NY,)), dma((NY,)), dma((NZ,)), dma((NZ,)),
        dma((NY,)), dma((NY,)), dma((NZ,)), dma((NZ,)),
        dma((8,)), dma((8,)), dma((8,)), dma((8,)),
    ]
    return pl.pallas_call(
        kernel,
        out_shape=outs,
        in_specs=[ANY_SPEC] * 8,
        out_specs=[ANY_SPEC] * 4,
        scratch_shapes=scratch,
        compiler_params=pltpu.CompilerParams(
            collective_id=1, has_side_effects=True, vmem_limit_bytes=56 * 2**20
        ),
        cost_estimate=pl.CostEstimate(
            flops=2700000000, bytes_accessed=8 * 2**20, transcendentals=100000
        ),
    )(*args)


STEPS = 4


def scale_kernel(
    ig_ref, gin_ref, gout_ref, vec_ref,
    ig_out, uin_ref, uout_ref, rin_out, cin_out, rout_out, cout_out,
):
    @pl.when(pl.program_id(0) == 0)
    def _():
        ig_out[...] = ig_ref[...]
        rin_out[...] = fold_lanes(vec_ref[0:1, :], 8)
        cout_out[...] = fold_lanes(vec_ref[1:2, :], 8)
        cin_out[...] = fold_lanes(vec_ref[2:3, 0:512], 4)
        rout_out[...] = fold_lanes(vec_ref[2:3, 512:1024], 4)

    inv_in = vec_ref[3:4, 0:512]
    inv_out = vec_ref[3:4, 512:1024]
    uin_ref[...] = (gin_ref[...] * inv_in).astype(BF16)
    for k in range(2):
        lanes = slice(k * 512, (k + 1) * 512)
        uout_ref[:, lanes] = (gout_ref[:, lanes] * inv_out).astype(BF16)


def scale(*args):
    shape = jax.ShapeDtypeStruct
    whole = lambda *dims: pl.BlockSpec(dims, lambda j: (0, 0))
    big = lambda *dims: pl.BlockSpec(dims, lambda j: (j, 0))
    return pl.pallas_call(
        scale_kernel,
        grid=(STEPS,),
        in_specs=[
            whole(8, 1024), big(1024 // STEPS, 512), big(512 // STEPS, 1024), whole(8, 1024),
        ],
        out_specs=[
            whole(8, 1024), big(1024 // STEPS, 512), big(512 // STEPS, 1024),
            whole(8, 128), whole(4, 128), whole(4, 128), whole(8, 128),
        ],
        out_shape=(
            shape((8, 1024), BF16), shape((1024, 512), BF16), shape((512, 1024), BF16),
            shape((8, 128), F32), shape((4, 128), F32), shape((4, 128), F32), shape((8, 128), F32),
        ),
        compiler_params=pltpu.CompilerParams(vmem_limit_bytes=56 * 2**20),
    )(*args)


def per_device(inputs, out_grad, w_in, w_out, row_in, col_in, row_out, col_out):
    line = lambda v: v.reshape(1, -1)
    whole = step(
        inputs, out_grad, w_in, w_out, line(row_in), line(col_in), line(row_out), line(col_out)
    )
    ig, update_in, update_out, rin, cin, rout, cout = scale(*whole)
    return (
        ig, update_in, update_out,
        rin.reshape(-1), cin.reshape(-1), rout.reshape(-1), cout.reshape(-1),
    )


def solution(mesh):
    placed = (
        P("mp", "narrow"),
        P("mp", "narrow"),
        P("narrow", "mp"),
        P("mp", "narrow"),
        P("narrow"),
        P("mp"),
        P("mp"),
        P("narrow"),
    )
    return jax.shard_map(
        per_device,
        mesh=mesh,
        in_specs=placed,
        out_specs=(
            P("mp", "narrow"),
            P("narrow", "mp"),
            P("mp", "narrow"),
            P("narrow"),
            P("mp"),
            P("mp"),
            P("narrow"),
        ),
        check_vma=False,
    )
```

```python
import functools

import jax
import jax.numpy as jnp
from jax import lax
from jax.experimental import pallas as pl
from jax.experimental.pallas import tpu as pltpu
from jax.sharding import PartitionSpec as P

D = 8192
FF = 32768
DECAY = 0.8
EPS = 1e-06
CLIP = 0.01

NY, NZ, NX = 4, 16, 4
F32, BF16 = jnp.float32, jnp.bfloat16
MESH = pl.DeviceIdType.MESH
EXACT = lax.Precision.HIGHEST
LAG = (1, 3, 5, 7)
FIRST = 256
FAR_FIRST = (8, 7, 9, 6, 10, 5, 11, 4, 12, 3, 13, 2, 14, 1, 15)


def dot(a, b, dims, precision=None):
    return lax.dot_general(
        a, b, ((dims[0], dims[1]), ((), ())), precision=precision, preferred_element_type=F32
    )


def fold_lanes(row, parts):
    return jnp.concatenate([row[:, k * 128 : (k + 1) * 128] for k in range(parts)], axis=0)


def unfold_lanes(block, start, parts):
    return jnp.concatenate([block[start + k : start + k + 1, :] for k in range(parts)], axis=1)


def lane_fold(q):
    out = q[:, 0:128]
    for k in range(1, q.shape[1] // 128):
        out = out + q[:, k * 128 : (k + 1) * 128]
    return out


def columns_of(row):
    return jnp.transpose(jnp.broadcast_to(row, (128, row.shape[1])))


def kernel(
    x_hbm, dy_hbm, win_hbm, wout_hbm, rin_hbm, cin_hbm, rout_hbm, cout_hbm,
    ig_hbm, gin_hbm, gout_hbm, vec_hbm,
    x_ref, dy_ref, win_ref, wout_ref, rin_ref, cin_ref, rout_ref, cout_ref,
    ig_ref, gin_ref, gout_ref, vec_ref,
    g1, g2, xs, ds, acts, hgs, keep, give, cx, tot, sx, xr, hh,
    ys, yr, zs, zr,
    rp_in, rp_out, cs_in, cs_out,
    my, mz, ty, tz, nb, nn,
    w_sem, o_sem,
    yg_s, yg_r, zg_s, zg_r, y2_s, y2_r, z2_s, z2_r, cx_s, cx_r, xr_s, xr_r, xg_s, xg_r,
    yi_s, yi_r, zi_s, zi_r, my_s, my_r, mz_s, mz_r, ty_s, ty_r, tz_s, tz_r,
    nb_s, nb_r, nn_s, nn_r,
):
    mp = lax.axis_index("mp")
    nar = lax.axis_index("narrow")
    y, z = mp // NZ, lax.rem(mp, NZ)
    x, c = nar // 2, lax.rem(nar, 2)

    def at_y(d):
        return (lax.rem(y + d, NY) * NZ + z, nar)

    def at_z(d):
        return (y * NZ + lax.rem(z + d, NZ), nar)

    def at_x(d):
        return (mp, lax.rem(x + d, NX) * 2 + c)

    def at_n(d):
        return (mp, lax.rem(nar + d, 8))

    other = (mp, x * 2 + 1 - c)

    def remote(src, dst, ssem, rsem, dev):
        return pltpu.make_async_remote_copy(
            src_ref=src, dst_ref=dst, send_sem=ssem, recv_sem=rsem,
            device_id=dev, device_id_type=MESH,
        )

    barrier = pltpu.get_barrier_semaphore()
    greet = [at_y(1), at_y(2), at_y(3), at_z(1), at_z(NZ - 1), at_z(2), at_z(NZ - 2), at_x(1), at_x(2), at_x(3), other]
    for dev in greet:
        pl.semaphore_signal(barrier, inc=1, device_id=dev, device_id_type=MESH)

    loads = [
        pltpu.make_async_copy(src, dst, w_sem.at[k])
        for k, (src, dst) in enumerate((
            (x_hbm, x_ref), (dy_hbm, dy_ref), (win_hbm, win_ref), (wout_hbm, wout_ref),
            (rin_hbm, rin_ref), (cin_hbm, cin_ref), (rout_hbm, rout_ref), (cout_hbm, cout_ref),
        ))
    ]
    for load in loads:
        load.start()
    loads[0].wait()
    loads[1].wait()
    mine = jnp.concatenate([x_ref[...].astype(F32), dy_ref[...].astype(F32)], axis=0).astype(BF16)
    g1[z, y] = mine[:, 0:FIRST]
    g2[z, y] = mine[:, FIRST:1024]
    vec_ref[...] = jnp.zeros_like(vec_ref)
    pl.semaphore_wait(barrier, len(greet))

    def y_copy(d):
        return remote(g1.at[z, y], g1.at[z, y], yg_s.at[d], yg_r.at[d], at_y(d))

    def z_way(way, r):
        hop = jnp.where(r > 1, 2, 1)
        back = r - hop
        row = lax.rem(z + (NZ - back if way == 0 else back), NZ)
        return row, at_z(hop if way == 0 else NZ - hop)

    def z_copy(way, r, k):
        row, dev = z_way(way, r)
        ref = g1.at[row, lax.rem(y + NY - k, NY)]
        return remote(ref, ref, zg_s.at[way, r, k], zg_r.at[way, r, k], dev)

    def z2_copy(way, r):
        row, dev = z_way(way, r)
        ref = g2.at[row, y]
        return remote(ref, ref, z2_s.at[way, r], z2_r.at[way, r], dev)

    def y2_copy(way, s, d):
        row = lax.rem(z + (NZ - s if way == 0 else s), NZ)
        ref = g2.at[row, y]
        return remote(ref, ref, y2_s.at[way, s, d], y2_r.at[way, s, d], at_y(d))

    def pair(s):
        first = lax.rem(z + NZ - s, NZ)
        second = lax.rem(z + lax.rem(s, 8), NZ)
        return jnp.where(c == 0, first, second), jnp.where(c == 0, second, first)

    def rows32(cell):
        return pl.ds(pl.multiple_of(cell * 32, 32), 32)

    def split16(block, width):
        block = block.astype(F32)
        return (
            block[:, 0:8, :].reshape(32, width).astype(BF16),
            block[:, 8:16, :].reshape(32, width).astype(BF16),
        )

    def cx_copy(s):
        i = s - 1
        return remote(give.at[i], cx.at[i], cx_s.at[i], cx_r.at[i], other)

    def xr_copy(s, d):
        i = s - 1
        to = lax.rem(x + d, NX)
        return remote(sx.at[i, to], xr.at[i, x], xr_s.at[i, d], xr_r.at[i, d], at_x(d))

    def xg_copy(s, k):
        d, flip = k // 2, k % 2
        ref = hh.at[pair(s)[0], x]
        core = 1 - c if flip else c
        dev = (mp, lax.rem(x + d, NX) * 2 + core)
        return remote(ref, ref, xg_s.at[s - 1, k], xg_r.at[s - 1, k], dev)

    def yi_copy(s, d):
        i = s - 1
        to = lax.rem(y + d, NY)
        return remote(ys.at[i, to], yr.at[i, y], yi_s.at[i, d], yi_r.at[i, d], at_y(d))

    def zi_copy(d):
        to = lax.rem(z + d, NZ)
        return remote(zs.at[to], zr.at[z], zi_s.at[d], zi_r.at[d], at_z(d))

    def project(s):
        cells = pair(s)
        got = []
        for cell in cells:
            low, high = split16(g1[cell], FIRST), split16(g2[cell], 1024 - FIRST)
            got.append([jnp.concatenate([a, b], axis=1) for a, b in zip(low, high)])
        xb = jnp.concatenate([g[0] for g in got], axis=0)
        db = jnp.concatenate([g[1] for g in got], axis=0)
        pre = dot(xb, win_ref[...], ((1,), (0,)))
        up = dot(db, wout_ref[...], ((1,), (1,)))
        i = s - 1
        keep[i, 0] = pre[0:32]
        keep[i, 1] = up[0:32]
        give[i, 0] = pre[32:64]
        give[i, 1] = up[32:64]
        cx_copy(s).start()
        for g, cell in zip(got, cells):
            xs[rows32(cell), :] = g[0]
            ds[rows32(cell), :] = g[1]

    def spread(s):
        i = s - 1
        cx_copy(s).wait_recv()
        t = keep[i] + cx[i]
        t = jnp.concatenate([t[0].reshape(4, 8, 512), t[1].reshape(4, 8, 512)], axis=1)
        tot[i] = t
        sx[i] = t.astype(BF16)
        for d in (2, 1, 3):
            xr_copy(s, d).start()

    def activate(s):
        i = s - 1
        t = tot[i, x]
        for d in (1, 3, 2):
            xr_copy(s, d).wait_recv()
            t = t + xr[i, lax.rem(x + NX - d, NX)].astype(F32)
        pre, up = t[0:8], t[8:16]
        sig = 1.0 / (1.0 + jnp.exp(-pre))
        hh[pair(s)[0], x] = jnp.concatenate(
            [pre * sig, up * (sig * (1.0 + pre * (1.0 - sig)))], axis=0
        ).astype(BF16)
        for k in (4, 5, 2, 6, 3, 7, 1):
            xg_copy(s, k).start()

    def back_project(s):
        for k in range(1, 8):
            xg_copy(s, k).wait_recv()
        cells = pair(s)
        got = [split16(hh[cell], 512) for cell in cells]
        p = dot(jnp.concatenate([g[1] for g in got], axis=0), win_ref[...], ((1,), (1,)))
        p = p.reshape(2, 4, 8, 1024)
        p = jnp.concatenate([p[..., 0:512], p[..., 512:1024]], axis=2).astype(BF16)
        for k in range(NY):
            ys[s - 1, k] = p[:, k]
        for d in (2, 1, 3):
            yi_copy(s, d).start()
        for g, cell in zip(got, cells):
            acts[rows32(cell), :] = g[0]
            hgs[rows32(cell), :] = g[1]

    def deliver(s):
        i = s - 1
        yr[i, y] = ys[i, y]
        for d in (1, 3, 2):
            yi_copy(s, d).wait_recv()
        t = (yr[i, 0].astype(F32) + yr[i, 1].astype(F32)) + (
            yr[i, 2].astype(F32) + yr[i, 3].astype(F32)
        )
        for k, cell in enumerate(pair(s)):
            zs[cell] = t[k].astype(BF16)

        zi_copy(NZ - s).start()

        @pl.when(s < 8)
        def _():
            zi_copy(lax.rem(s, NZ)).start()

    for d in (2, 1, 3):
        y_copy(d).start()
    for r in (2, 1):
        for way in range(2):
            z2_copy(way, r).start()
            z_copy(way, r, 0).start()
    for k in (1, 3, 2):
        y_copy(k).wait_recv()
        for r in (2, 1):
            for way in range(2):
                z_copy(way, r, k).start()
    for r in (1, 2):
        for way in range(2):
            z2_copy(way, r).wait_recv()
            z2_copy(way, r + 2).start()
            for d in (2, 1, 3):
                y2_copy(way, r, d).start()
    for d in (2, 1, 3):
        y2_copy(0, 0, d).start()
    for load in loads[2:]:
        load.wait()

    @pl.loop(1, 8 + LAG[2] + 1)
    def _(s):
        @pl.when(s < 6)
        def _():
            for k in (0, 1, 3, 2):
                for way in range(2):
                    z_copy(way, s, k).wait_recv()
                    z_copy(way, s + 2, k).start()
            for way in range(2):
                z2_copy(way, s + 2).wait_recv()
                if way == 0:

                    @pl.when(s < 5)
                    def _():
                        z2_copy(0, s + 4).start()
                else:

                    @pl.when(s < 4)
                    def _():
                        z2_copy(1, s + 4).start()

                for d in (2, 1, 3):
                    y2_copy(way, s + 2, d).start()

        @pl.when(s == 6)
        def _():
            for k in (0, 1, 3, 2):
                for way in range(2):
                    z_copy(way, 6, k).wait_recv()
                    if (k < 2) == (way == 0):
                        z_copy(way, 8, k).start()
            z2_copy(0, 8).wait_recv()
            for d in (2, 1, 3):
                y2_copy(0, 8, d).start()

        @pl.when(s == 7)
        def _():
            for k in (0, 1, 3, 2):
                for way in range(2):
                    z_copy(way, 7, k).wait_recv()

        @pl.when(s < 8)
        def _():
            for way in range(2):
                for d in (1, 3, 2):
                    y2_copy(way, s, d).wait_recv()

        @pl.when(s == 8)
        def _():
            for k in (0, 1, 3, 2):
                z_copy(0 if k < 2 else 1, 8, k).wait_recv()
            for d in (1, 3, 2):
                y2_copy(0, 0, d).wait_recv()
                y2_copy(0, 8, d).wait_recv()

        def stage(lag, run):
            @pl.when(jnp.logical_and(s > lag, s <= 8 + lag))
            def _():
                run(s - lag)

        stage(LAG[0], spread)
        stage(LAG[1], activate)

        @pl.when(s <= 8)
        def _():
            project(s)

        stage(LAG[2], back_project)
        stage(LAG[3], deliver)

    rp_out[...] = jnp.zeros_like(rp_out)
    cs_in[...] = jnp.zeros_like(cs_in)

    @pl.loop(0, 4)
    def _(j):
        cols = pl.ds(pl.multiple_of(j * 256, 256), 256)
        g = dot(acts[...], ds[:, cols], ((0,), (0,)))
        gout_ref[:, cols] = g
        q = g * g
        cs_out[:, cols] = jnp.sum(q, axis=0, keepdims=True)
        rp_out[...] += lane_fold(q)
        g = dot(xs[:, cols], hgs[...], ((0,), (0,)))
        gin_ref[cols, :] = g
        q = g * g
        cs_in[...] += jnp.sum(q, axis=0, keepdims=True)
        rp_in[cols, :] = lane_fold(q)

    save_in = pltpu.make_async_copy(gin_ref, gin_hbm, o_sem.at[0])
    save_out = pltpu.make_async_copy(gout_ref, gout_hbm, o_sem.at[1])
    save_ig = pltpu.make_async_copy(ig_ref, ig_hbm, o_sem.at[2])
    save_vec = pltpu.make_async_copy(vec_ref, vec_hbm, o_sem.at[3])
    ones = jnp.ones((8, 128), F32)

    def my_copy(d):
        return remote(my.at[y], my.at[y], my_s.at[d], my_r.at[d], at_y(d))

    def mz_copy(d):
        return remote(mz.at[z], mz.at[z], mz_s.at[d], mz_r.at[d], at_z(d))

    def ty_copy(d):
        return remote(ty.at[y], ty.at[y], ty_s.at[d], ty_r.at[d], at_y(d))

    def tz_copy(d):
        return remote(tz.at[z], tz.at[z], tz_s.at[d], tz_r.at[d], at_z(d))

    def nb_copy(d):
        return remote(nb.at[nar], nb.at[nar], nb_s.at[d], nb_r.at[d], at_n(d))

    def nn_copy(d):
        return remote(nn.at[nar], nn.at[nar], nn_s.at[d], nn_r.at[d], at_n(d))

    row_sums_out = dot(ones, rp_out[...], ((1,), (1,)), EXACT)[0:1]
    nb[nar] = jnp.concatenate([fold_lanes(cs_in[...], 4), fold_lanes(row_sums_out, 4)], axis=0)
    for d in range(1, 8):
        nb_copy(d).start()
    row_sums_in = dot(ones, rp_in[...], ((1,), (1,)), EXACT)[0:1]
    my[y] = jnp.concatenate([fold_lanes(row_sums_in, 8), fold_lanes(cs_out[...], 8)], axis=0)
    for d in range(1, NY):
        my_copy(d).start()

    for s in range(8 + LAG[2] - LAG[3] + 1, 9):
        deliver(s)
    zr[z] = zs[z]

    for d in range(1, 8):
        nb_copy(d).wait_recv()
    n_sum = nb[0]
    for k in range(1, 8):
        n_sum = n_sum + nb[k]
    cin_new = DECAY * cin_ref[...] + (1.0 - DECAY) * (unfold_lanes(n_sum, 0, 4) / D + EPS)
    rout_new = DECAY * rout_ref[...] + (1.0 - DECAY) * (unfold_lanes(n_sum, 4, 4) / D + EPS)
    vec_ref[2:3, 0:512] = cin_new
    vec_ref[2:3, 512:1024] = rout_new

    inv_cin = 1.0 / cin_new
    rp_out[...] = columns_of(1.0 / rout_new)

    @pl.loop(0, 4)
    def _(j):
        cols = pl.ds(pl.multiple_of(j * 256, 256), 256)
        g = gout_ref[:, cols]
        q = g * g
        w = rp_out[...]
        q = jnp.concatenate([q[:, 0:128] * w, q[:, 128:256] * w], axis=1)
        cs_out[:, cols] = jnp.sum(q, axis=0, keepdims=True)
        g = gin_ref[cols, :]
        rp_in[cols, :] = lane_fold(g * g * inv_cin)

    t_in = dot(ones, rp_in[...], ((1,), (1,)), EXACT)[0:1]
    ty[y] = jnp.concatenate([fold_lanes(t_in, 8), fold_lanes(cs_out[...], 8)], axis=0)
    for d in range(1, NY):
        ty_copy(d).start()

    for d in range(1, NY):
        my_copy(d).wait_recv()
    mz[z] = ((my[0] + my[1]) + (my[2] + my[3])).astype(BF16)

    for d in FAR_FIRST:
        mz_copy(d).start()

    for d in range(1, NY):
        ty_copy(d).wait_recv()
    tz[z] = ((ty[0] + ty[1]) + (ty[2] + ty[3])).astype(BF16)

    for d in FAR_FIRST:
        tz_copy(d).start()

    @pl.loop(1, NZ)
    def _(d):
        zi_copy(d).wait_recv()

    t = zr[0].astype(F32)
    for k in range(1, NZ):
        t = t + zr[k].astype(F32)
    ig_ref[...] = jnp.concatenate([t[0:8], t[8:16]], axis=1).astype(BF16)
    save_ig.start()

    @pl.loop(1, NZ)
    def _(d):
        mz_copy(d).wait_recv()

    m_sum = mz[0].astype(F32)
    for k in range(1, NZ):
        m_sum = m_sum + mz[k].astype(F32)
    r_new = DECAY * rin_ref[...] + (1.0 - DECAY) * (unfold_lanes(m_sum, 0, 8) / FF + EPS)
    c_new = DECAY * cout_ref[...] + (1.0 - DECAY) * (unfold_lanes(m_sum, 8, 8) / FF + EPS)
    vec_ref[0:1, :] = r_new
    vec_ref[1:2, :] = c_new
    inv_r, inv_c = fold_lanes(1.0 / r_new, 8), fold_lanes(1.0 / c_new, 8)

    rp_in[...] = columns_of(r_new)
    rp_out[...] = columns_of(rout_new)

    @pl.loop(0, 8)
    def _(j):
        rows = pl.ds(pl.multiple_of(j * 128, 128), 128)
        r = rp_in[rows, :]
        for k in range(4):
            lanes = slice(k * 128, (k + 1) * 128)
            gin_ref[rows, lanes] = gin_ref[rows, lanes] * lax.rsqrt(r * vec_ref[2:3, lanes])
        rows = pl.ds(pl.multiple_of(j * 64, 64), 64)
        r = rp_out[rows, :]
        for k in range(8):
            lanes = slice(k * 128, (k + 1) * 128)
            gout_ref[rows, lanes] = gout_ref[rows, lanes] * lax.rsqrt(r * vec_ref[1:2, lanes])

    save_in.start()
    save_out.start()

    @pl.loop(1, NZ)
    def _(d):
        tz_copy(d).wait_recv()

    t = tz[0].astype(F32)
    for k in range(1, NZ):
        t = t + tz[k].astype(F32)
    n_in = jnp.sum(t[0:8] * inv_r, axis=0, keepdims=True)
    n_out = jnp.sum(t[8:16] * inv_c, axis=0, keepdims=True)
    which = lax.broadcasted_iota(jnp.int32, (8, 128), 0)
    nn[nar] = jnp.where(which < 4, n_in, n_out)
    for d in range(1, 8):
        nn_copy(d).start()
    for d in range(1, 8):
        nn_copy(d).wait_recv()
    t = nn[0]
    for k in range(1, 8):
        t = t + nn[k]
    total = jnp.sum(t, axis=1, keepdims=True)
    inv = 1.0 / jnp.maximum(CLIP, jnp.sqrt(total / (float(D) * float(FF))))
    vec_ref[3:4, 0:512] = jnp.broadcast_to(inv[0:1], (1, 512))
    vec_ref[3:4, 512:1024] = jnp.broadcast_to(inv[4:5], (1, 512))
    save_vec.start()

    for d in range(1, NY):
        y_copy(d).wait_send()
        my_copy(d).wait_send()
        ty_copy(d).wait_send()

    @pl.loop(1, 9)
    def _(s):
        cx_copy(s).wait_send()
        for k in range(1, 8):
            xg_copy(s, k).wait_send()
        for d in range(1, NX):
            xr_copy(s, d).wait_send()
            yi_copy(s, d).wait_send()

    for d in range(1, 8):
        nb_copy(d).wait_send()
        nn_copy(d).wait_send()

    @pl.loop(1, 8)
    def _(s):
        for way in range(2):
            z2_copy(way, s).wait_send()
            for k in range(NY):
                z_copy(way, s, k).wait_send()
            for d in range(1, NY):
                y2_copy(way, s, d).wait_send()

    for k in range(NY):
        z_copy(0 if k < 2 else 1, 8, k).wait_send()
    z2_copy(0, 8).wait_send()
    for d in range(1, NY):
        y2_copy(0, 0, d).wait_send()
        y2_copy(0, 8, d).wait_send()

    @pl.loop(1, NZ)
    def _(d):
        mz_copy(d).wait_send()
        tz_copy(d).wait_send()
        zi_copy(d).wait_send()

    for save in (save_in, save_out, save_ig, save_vec):
        save.wait()


ANY_SPEC = pl.BlockSpec(memory_space=pl.ANY)


def step(*args):
    dma = pltpu.SemaphoreType.DMA
    vmem = pltpu.VMEM
    shape = jax.ShapeDtypeStruct
    outs = (
        shape((8, 1024), BF16), shape((1024, 512), F32), shape((512, 1024), F32),
        shape((8, 1024), F32),
    )
    scratch = [
        vmem((8, 1024), BF16), vmem((8, 1024), BF16), vmem((1024, 512), BF16), vmem((512, 1024), BF16),
        vmem((1, 1024), F32), vmem((1, 512), F32), vmem((1, 512), F32), vmem((1, 1024), F32),
        vmem((8, 1024), BF16), vmem((1024, 512), F32), vmem((512, 1024), F32), vmem((8, 1024), F32),
        vmem((NZ, NY, 16, FIRST), BF16), vmem((NZ, NY, 16, 1024 - FIRST), BF16),
        vmem((512, 1024), BF16), vmem((512, 1024), BF16),
        vmem((512, 512), BF16), vmem((512, 512), BF16),
        vmem((8, 2, 32, 512), F32), vmem((8, 2, 32, 512), F32), vmem((8, 2, 32, 512), F32),
        vmem((8, NX, 16, 512), F32), vmem((8, NX, 16, 512), BF16), vmem((8, NX, 16, 512), BF16),
        vmem((NZ, NX, 16, 512), BF16),
        vmem((8, NY, 2, 16, 512), BF16), vmem((8, NY, 2, 16, 512), BF16),
        vmem((NZ, 16, 512), BF16), vmem((NZ, 16, 512), BF16),
        vmem((1024, 128), F32), vmem((512, 128), F32), vmem((1, 512), F32), vmem((1, 1024), F32),
        vmem((NY, 16, 128), F32), vmem((NZ, 16, 128), BF16),
        vmem((NY, 16, 128), F32), vmem((NZ, 16, 128), BF16),
        vmem((8, 8, 128), F32), vmem((8, 8, 128), F32),
        dma((8,)), dma((4,)),
        dma((NY,)), dma((NY,)), dma((2, 9, NY)), dma((2, 9, NY)),
        dma((2, 9, NY)), dma((2, 9, NY)), dma((2, 9)), dma((2, 9)), dma((8,)), dma((8,)),
        dma((8, NX)), dma((8, NX)), dma((8, 8)), dma((8, 8)),
        dma((8, NY)), dma((8, NY)), dma((NZ,)), dma((NZ,)),
        dma((NY,)), dma((NY,)), dma((NZ,)), dma((NZ,)),
        dma((NY,)), dma((NY,)), dma((NZ,)), dma((NZ,)),
        dma((8,)), dma((8,)), dma((8,)), dma((8,)),
    ]
    return pl.pallas_call(
        kernel,
        out_shape=outs,
        in_specs=[ANY_SPEC] * 8,
        out_specs=[ANY_SPEC] * 4,
        scratch_shapes=scratch,
        compiler_params=pltpu.CompilerParams(
            collective_id=1, has_side_effects=True, vmem_limit_bytes=56 * 2**20
        ),
        cost_estimate=pl.CostEstimate(
            flops=2700000000, bytes_accessed=8 * 2**20, transcendentals=100000
        ),
    )(*args)


STEPS = 2


def scale_kernel(
    ig_ref, gin_ref, gout_ref, vec_ref,
    ig_out, uin_ref, uout_ref, rin_out, cin_out, rout_out, cout_out,
):
    @pl.when(pl.program_id(0) == 0)
    def _():
        ig_out[...] = ig_ref[...]
        rin_out[...] = fold_lanes(vec_ref[0:1, :], 8)
        cout_out[...] = fold_lanes(vec_ref[1:2, :], 8)
        cin_out[...] = fold_lanes(vec_ref[2:3, 0:512], 4)
        rout_out[...] = fold_lanes(vec_ref[2:3, 512:1024], 4)

    inv_in = vec_ref[3:4, 0:512]
    inv_out = vec_ref[3:4, 512:1024]
    uin_ref[...] = (gin_ref[...] * inv_in).astype(BF16)
    for k in range(2):
        lanes = slice(k * 512, (k + 1) * 512)
        uout_ref[:, lanes] = (gout_ref[:, lanes] * inv_out).astype(BF16)


def scale(*args):
    shape = jax.ShapeDtypeStruct
    whole = lambda *dims: pl.BlockSpec(dims, lambda j: (0, 0))
    big = lambda *dims: pl.BlockSpec(dims, lambda j: (j, 0))
    return pl.pallas_call(
        scale_kernel,
        grid=(STEPS,),
        in_specs=[
            whole(8, 1024), big(1024 // STEPS, 512), big(512 // STEPS, 1024), whole(8, 1024),
        ],
        out_specs=[
            whole(8, 1024), big(1024 // STEPS, 512), big(512 // STEPS, 1024),
            whole(8, 128), whole(4, 128), whole(4, 128), whole(8, 128),
        ],
        out_shape=(
            shape((8, 1024), BF16), shape((1024, 512), BF16), shape((512, 1024), BF16),
            shape((8, 128), F32), shape((4, 128), F32), shape((4, 128), F32), shape((8, 128), F32),
        ),
        compiler_params=pltpu.CompilerParams(vmem_limit_bytes=56 * 2**20),
    )(*args)


def per_device(inputs, out_grad, w_in, w_out, row_in, col_in, row_out, col_out):
    line = lambda v: v.reshape(1, -1)
    whole = step(
        inputs, out_grad, w_in, w_out, line(row_in), line(col_in), line(row_out), line(col_out)
    )
    ig, update_in, update_out, rin, cin, rout, cout = scale(*whole)
    return (
        ig, update_in, update_out,
        rin.reshape(-1), cin.reshape(-1), rout.reshape(-1), cout.reshape(-1),
    )


def solution(mesh):
    placed = (
        P("mp", "narrow"),
        P("mp", "narrow"),
        P("narrow", "mp"),
        P("mp", "narrow"),
        P("narrow"),
        P("mp"),
        P("mp"),
        P("narrow"),
    )
    return jax.shard_map(
        per_device,
        mesh=mesh,
        in_specs=placed,
        out_specs=(
            P("mp", "narrow"),
            P("narrow", "mp"),
            P("mp", "narrow"),
            P("narrow"),
            P("mp"),
            P("mp"),
            P("narrow"),
        ),
        check_vma=False,
    )
```

```python
import functools

import jax
import jax.numpy as jnp
from jax import lax
from jax.experimental import pallas as pl
from jax.experimental.pallas import tpu as pltpu
from jax.sharding import PartitionSpec as P

D = 8192
FF = 32768
DECAY = 0.8
EPS = 1e-06
CLIP = 0.01

NY, NZ, NX = 4, 16, 4
F32, BF16 = jnp.float32, jnp.bfloat16
MESH = pl.DeviceIdType.MESH
EXACT = lax.Precision.HIGHEST
LAG = (1, 3, 5, 7)
FIRST = 256
FAR_FIRST = (8, 7, 9, 6, 10, 5, 11, 4, 12, 3, 13, 2, 14, 1, 15)


def dot(a, b, dims, precision=None):
    return lax.dot_general(
        a, b, ((dims[0], dims[1]), ((), ())), precision=precision, preferred_element_type=F32
    )


def fold_lanes(row, parts):
    return jnp.concatenate([row[:, k * 128 : (k + 1) * 128] for k in range(parts)], axis=0)


def unfold_lanes(block, start, parts):
    return jnp.concatenate([block[start + k : start + k + 1, :] for k in range(parts)], axis=1)


def lane_fold(q):
    out = q[:, 0:128]
    for k in range(1, q.shape[1] // 128):
        out = out + q[:, k * 128 : (k + 1) * 128]
    return out


def columns_of(row):
    return jnp.transpose(jnp.broadcast_to(row, (128, row.shape[1])))


def kernel(
    x_hbm, dy_hbm, win_hbm, wout_hbm, rin_hbm, cin_hbm, rout_hbm, cout_hbm,
    ig_hbm, gin_hbm, gout_hbm, vec_hbm,
    x_ref, dy_ref, win_ref, wout_ref, rin_ref, cin_ref, rout_ref, cout_ref,
    ig_ref, gin_ref, gout_ref, vec_ref,
    g1, g2, xs, ds, acts, hgs, keep, give, cx, tot, sx, xr, hh,
    ys, yr, zs, zr,
    rp_in, rp_out, cs_in, cs_out,
    my, mz, ty, tz, nb, nn,
    w_sem, o_sem,
    yg_s, yg_r, zg_s, zg_r, y2_s, y2_r, z2_s, z2_r, cx_s, cx_r, xr_s, xr_r, xg_s, xg_r,
    yi_s, yi_r, zi_s, zi_r, my_s, my_r, mz_s, mz_r, ty_s, ty_r, tz_s, tz_r,
    nb_s, nb_r, nn_s, nn_r,
):
    mp = lax.axis_index("mp")
    nar = lax.axis_index("narrow")
    y, z = mp // NZ, lax.rem(mp, NZ)
    x, c = nar // 2, lax.rem(nar, 2)

    def at_y(d):
        return (lax.rem(y + d, NY) * NZ + z, nar)

    def at_z(d):
        return (y * NZ + lax.rem(z + d, NZ), nar)

    def at_x(d):
        return (mp, lax.rem(x + d, NX) * 2 + c)

    def at_n(d):
        return (mp, lax.rem(nar + d, 8))

    other = (mp, x * 2 + 1 - c)

    def remote(src, dst, ssem, rsem, dev):
        return pltpu.make_async_remote_copy(
            src_ref=src, dst_ref=dst, send_sem=ssem, recv_sem=rsem,
            device_id=dev, device_id_type=MESH,
        )

    barrier = pltpu.get_barrier_semaphore()
    greet = [at_y(1), at_y(2), at_y(3), at_z(1), at_z(NZ - 1), at_z(2), at_z(NZ - 2), at_x(1), at_x(2), at_x(3), other]
    for dev in greet:
        pl.semaphore_signal(barrier, inc=1, device_id=dev, device_id_type=MESH)

    loads = [
        pltpu.make_async_copy(src, dst, w_sem.at[k])
        for k, (src, dst) in enumerate((
            (x_hbm, x_ref), (dy_hbm, dy_ref), (win_hbm, win_ref), (wout_hbm, wout_ref),
            (rin_hbm, rin_ref), (cin_hbm, cin_ref), (rout_hbm, rout_ref), (cout_hbm, cout_ref),
        ))
    ]
    for load in loads:
        load.start()
    loads[0].wait()
    loads[1].wait()
    mine = jnp.concatenate([x_ref[...].astype(F32), dy_ref[...].astype(F32)], axis=0).astype(BF16)
    g1[z, y] = mine[:, 0:FIRST]
    g2[z, y] = mine[:, FIRST:1024]
    vec_ref[...] = jnp.zeros_like(vec_ref)
    pl.semaphore_wait(barrier, len(greet))

    def y_copy(d):
        return remote(g1.at[z, y], g1.at[z, y], yg_s.at[d], yg_r.at[d], at_y(d))

    def z_way(way, r):
        hop = jnp.where(r > 1, 2, 1)
        back = r - hop
        row = lax.rem(z + (NZ - back if way == 0 else back), NZ)
        return row, at_z(hop if way == 0 else NZ - hop)

    def z_copy(way, r, k):
        row, dev = z_way(way, r)
        ref = g1.at[row, lax.rem(y + NY - k, NY)]
        return remote(ref, ref, zg_s.at[way, r, k], zg_r.at[way, r, k], dev)

    def z2_copy(way, r):
        row, dev = z_way(way, r)
        ref = g2.at[row, y]
        return remote(ref, ref, z2_s.at[way, r], z2_r.at[way, r], dev)

    def y2_copy(way, s, d):
        row = lax.rem(z + (NZ - s if way == 0 else s), NZ)
        ref = g2.at[row, y]
        return remote(ref, ref, y2_s.at[way, s, d], y2_r.at[way, s, d], at_y(d))

    def pair(s):
        first = lax.rem(z + NZ - s, NZ)
        second = lax.rem(z + lax.rem(s, 8), NZ)
        return jnp.where(c == 0, first, second), jnp.where(c == 0, second, first)

    def rows32(cell):
        return pl.ds(pl.multiple_of(cell * 32, 32), 32)

    def split16(block, width):
        block = block.astype(F32)
        return (
            block[:, 0:8, :].reshape(32, width).astype(BF16),
            block[:, 8:16, :].reshape(32, width).astype(BF16),
        )

    def cx_copy(s):
        i = s - 1
        return remote(give.at[i], cx.at[i], cx_s.at[i], cx_r.at[i], other)

    def xr_copy(s, d):
        i = s - 1
        to = lax.rem(x + d, NX)
        return remote(sx.at[i, to], xr.at[i, x], xr_s.at[i, d], xr_r.at[i, d], at_x(d))

    def xg_copy(s, k):
        d, flip = k // 2, k % 2
        ref = hh.at[pair(s)[0], x]
        core = 1 - c if flip else c
        dev = (mp, lax.rem(x + d, NX) * 2 + core)
        return remote(ref, ref, xg_s.at[s - 1, k], xg_r.at[s - 1, k], dev)

    def yi_copy(s, d):
        i = s - 1
        to = lax.rem(y + d, NY)
        return remote(ys.at[i, to], yr.at[i, y], yi_s.at[i, d], yi_r.at[i, d], at_y(d))

    def zi_copy(d):
        to = lax.rem(z + d, NZ)
        return remote(zs.at[to], zr.at[z], zi_s.at[d], zi_r.at[d], at_z(d))

    def project(s):
        cells = pair(s)
        got = []
        for cell in cells:
            low, high = split16(g1[cell], FIRST), split16(g2[cell], 1024 - FIRST)
            got.append([jnp.concatenate([a, b], axis=1) for a, b in zip(low, high)])
        xb = jnp.concatenate([g[0] for g in got], axis=0)
        db = jnp.concatenate([g[1] for g in got], axis=0)
        pre = dot(xb, win_ref[...], ((1,), (0,)))
        up = dot(db, wout_ref[...], ((1,), (1,)))
        i = s - 1
        keep[i, 0] = pre[0:32]
        keep[i, 1] = up[0:32]
        give[i, 0] = pre[32:64]
        give[i, 1] = up[32:64]
        cx_copy(s).start()
        for g, cell in zip(got, cells):
            xs[rows32(cell), :] = g[0]
            ds[rows32(cell), :] = g[1]

    def spread(s):
        i = s - 1
        cx_copy(s).wait_recv()
        t = keep[i] + cx[i]
        t = jnp.concatenate([t[0].reshape(4, 8, 512), t[1].reshape(4, 8, 512)], axis=1)
        tot[i] = t
        sx[i] = t.astype(BF16)
        for d in (2, 1, 3):
            xr_copy(s, d).start()

    def activate(s):
        i = s - 1
        t = tot[i, x]
        for d in (1, 3, 2):
            xr_copy(s, d).wait_recv()
            t = t + xr[i, lax.rem(x + NX - d, NX)].astype(F32)
        pre, up = t[0:8], t[8:16]
        sig = 1.0 / (1.0 + jnp.exp(-pre))
        hh[pair(s)[0], x] = jnp.concatenate(
            [pre * sig, up * (sig * (1.0 + pre * (1.0 - sig)))], axis=0
        ).astype(BF16)
        for k in (4, 5, 2, 6, 3, 7, 1):
            xg_copy(s, k).start()

    def back_project(s):
        for k in range(1, 8):
            xg_copy(s, k).wait_recv()
        cells = pair(s)
        got = [split16(hh[cell], 512) for cell in cells]
        p = dot(jnp.concatenate([g[1] for g in got], axis=0), win_ref[...], ((1,), (1,)))
        p = p.reshape(2, 4, 8, 1024)
        p = jnp.concatenate([p[..., 0:512], p[..., 512:1024]], axis=2).astype(BF16)
        for k in range(NY):
            ys[s - 1, k] = p[:, k]
        for d in (2, 1, 3):
            yi_copy(s, d).start()
        for g, cell in zip(got, cells):
            acts[rows32(cell), :] = g[0]
            hgs[rows32(cell), :] = g[1]

    def deliver(s):
        i = s - 1
        yr[i, y] = ys[i, y]
        for d in (1, 3, 2):
            yi_copy(s, d).wait_recv()
        t = (yr[i, 0].astype(F32) + yr[i, 1].astype(F32)) + (
            yr[i, 2].astype(F32) + yr[i, 3].astype(F32)
        )
        for k, cell in enumerate(pair(s)):
            zs[cell] = t[k].astype(BF16)

        zi_copy(NZ - s).start()

        @pl.when(s < 8)
        def _():
            zi_copy(lax.rem(s, NZ)).start()

    for d in (2, 1, 3):
        y_copy(d).start()
    for r in (2, 1):
        for way in range(2):
            z2_copy(way, r).start()
            z_copy(way, r, 0).start()
    for k in (1, 3, 2):
        y_copy(k).wait_recv()
        for r in (2, 1):
            for way in range(2):
                z_copy(way, r, k).start()
    for r in (1, 2):
        for way in range(2):
            z2_copy(way, r).wait_recv()
            z2_copy(way, r + 2).start()
            for d in (2, 1, 3):
                y2_copy(way, r, d).start()
    for d in (2, 1, 3):
        y2_copy(0, 0, d).start()
    for load in loads[2:]:
        load.wait()

    @pl.loop(1, 8 + LAG[2] + 1)
    def _(s):
        @pl.when(s < 6)
        def _():
            for k in (0, 1, 3, 2):
                for way in range(2):
                    z_copy(way, s, k).wait_recv()
                    z_copy(way, s + 2, k).start()
            for way in range(2):
                z2_copy(way, s + 2).wait_recv()
                if way == 0:

                    @pl.when(s < 5)
                    def _():
                        z2_copy(0, s + 4).start()
                else:

                    @pl.when(s < 4)
                    def _():
                        z2_copy(1, s + 4).start()

                for d in (2, 1, 3):
                    y2_copy(way, s + 2, d).start()

        @pl.when(s == 6)
        def _():
            for k in (0, 1, 3, 2):
                for way in range(2):
                    z_copy(way, 6, k).wait_recv()
                    if (k < 2) == (way == 0):
                        z_copy(way, 8, k).start()
            z2_copy(0, 8).wait_recv()
            for d in (2, 1, 3):
                y2_copy(0, 8, d).start()

        @pl.when(s == 7)
        def _():
            for k in (0, 1, 3, 2):
                for way in range(2):
                    z_copy(way, 7, k).wait_recv()

        @pl.when(s < 8)
        def _():
            for way in range(2):
                for d in (1, 3, 2):
                    y2_copy(way, s, d).wait_recv()

        @pl.when(s == 8)
        def _():
            for k in (0, 1, 3, 2):
                z_copy(0 if k < 2 else 1, 8, k).wait_recv()
            for d in (1, 3, 2):
                y2_copy(0, 0, d).wait_recv()
                y2_copy(0, 8, d).wait_recv()

        def stage(lag, run):
            @pl.when(jnp.logical_and(s > lag, s <= 8 + lag))
            def _():
                run(s - lag)

        stage(LAG[0], spread)
        stage(LAG[1], activate)

        @pl.when(s <= 8)
        def _():
            project(s)

        stage(LAG[2], back_project)
        stage(LAG[3], deliver)

    rp_out[...] = jnp.zeros_like(rp_out)
    cs_in[...] = jnp.zeros_like(cs_in)

    @pl.loop(0, 4)
    def _(j):
        cols = pl.ds(pl.multiple_of(j * 256, 256), 256)
        g = dot(acts[...], ds[:, cols], ((0,), (0,)))
        gout_ref[:, cols] = g
        q = g * g
        cs_out[:, cols] = jnp.sum(q, axis=0, keepdims=True)
        rp_out[...] += lane_fold(q)
        g = dot(xs[:, cols], hgs[...], ((0,), (0,)))
        gin_ref[cols, :] = g
        q = g * g
        cs_in[...] += jnp.sum(q, axis=0, keepdims=True)
        rp_in[cols, :] = lane_fold(q)

    save_in = pltpu.make_async_copy(gin_ref, gin_hbm, o_sem.at[0])
    save_out = pltpu.make_async_copy(gout_ref, gout_hbm, o_sem.at[1])
    save_ig = pltpu.make_async_copy(ig_ref, ig_hbm, o_sem.at[2])
    save_vec = pltpu.make_async_copy(vec_ref, vec_hbm, o_sem.at[3])
    ones = jnp.ones((8, 128), F32)

    def my_copy(d):
        return remote(my.at[y], my.at[y], my_s.at[d], my_r.at[d], at_y(d))

    def mz_copy(d):
        return remote(mz.at[z], mz.at[z], mz_s.at[d], mz_r.at[d], at_z(d))

    def ty_copy(d):
        return remote(ty.at[y], ty.at[y], ty_s.at[d], ty_r.at[d], at_y(d))

    def tz_copy(d):
        return remote(tz.at[z], tz.at[z], tz_s.at[d], tz_r.at[d], at_z(d))

    def nb_copy(d):
        return remote(nb.at[nar], nb.at[nar], nb_s.at[d], nb_r.at[d], at_n(d))

    def nn_copy(d):
        return remote(nn.at[nar], nn.at[nar], nn_s.at[d], nn_r.at[d], at_n(d))

    row_sums_out = dot(ones, rp_out[...], ((1,), (1,)), EXACT)[0:1]
    nb[nar] = jnp.concatenate([fold_lanes(cs_in[...], 4), fold_lanes(row_sums_out, 4)], axis=0)
    for d in range(1, 8):
        nb_copy(d).start()
    row_sums_in = dot(ones, rp_in[...], ((1,), (1,)), EXACT)[0:1]
    my[y] = jnp.concatenate([fold_lanes(row_sums_in, 8), fold_lanes(cs_out[...], 8)], axis=0)
    for d in range(1, NY):
        my_copy(d).start()

    for s in range(8 + LAG[2] - LAG[3] + 1, 9):
        deliver(s)
    zr[z] = zs[z]

    for d in range(1, 8):
        nb_copy(d).wait_recv()
    n_sum = nb[0]
    for k in range(1, 8):
        n_sum = n_sum + nb[k]
    cin_new = DECAY * cin_ref[...] + (1.0 - DECAY) * (unfold_lanes(n_sum, 0, 4) / D + EPS)
    rout_new = DECAY * rout_ref[...] + (1.0 - DECAY) * (unfold_lanes(n_sum, 4, 4) / D + EPS)
    vec_ref[2:3, 0:512] = cin_new
    vec_ref[2:3, 512:1024] = rout_new

    inv_cin = 1.0 / cin_new
    rp_out[...] = columns_of(1.0 / rout_new)

    @pl.loop(0, 4)
    def _(j):
        cols = pl.ds(pl.multiple_of(j * 256, 256), 256)
        g = gout_ref[:, cols]
        q = g * g
        w = rp_out[...]
        q = jnp.concatenate([q[:, 0:128] * w, q[:, 128:256] * w], axis=1)
        cs_out[:, cols] = jnp.sum(q, axis=0, keepdims=True)
        g = gin_ref[cols, :]
        rp_in[cols, :] = lane_fold(g * g * inv_cin)

    t_in = dot(ones, rp_in[...], ((1,), (1,)), EXACT)[0:1]
    ty[y] = jnp.concatenate([fold_lanes(t_in, 8), fold_lanes(cs_out[...], 8)], axis=0)
    for d in range(1, NY):
        ty_copy(d).start()

    for d in range(1, NY):
        my_copy(d).wait_recv()
    mz[z] = ((my[0] + my[1]) + (my[2] + my[3])).astype(BF16)

    for d in FAR_FIRST:
        mz_copy(d).start()

    for d in range(1, NY):
        ty_copy(d).wait_recv()
    tz[z] = ((ty[0] + ty[1]) + (ty[2] + ty[3])).astype(BF16)

    for d in FAR_FIRST:
        tz_copy(d).start()

    for d in range(1, NY):
        y_copy(d).wait_send()
        my_copy(d).wait_send()
        ty_copy(d).wait_send()

    @pl.loop(1, 9)
    def _(s):
        cx_copy(s).wait_send()
        for k in range(1, 8):
            xg_copy(s, k).wait_send()
        for d in range(1, NX):
            xr_copy(s, d).wait_send()
            yi_copy(s, d).wait_send()

    for d in range(1, 8):
        nb_copy(d).wait_send()

    @pl.loop(1, 8)
    def _(s):
        for way in range(2):
            z2_copy(way, s).wait_send()
            for k in range(NY):
                z_copy(way, s, k).wait_send()
            for d in range(1, NY):
                y2_copy(way, s, d).wait_send()

    for k in range(NY):
        z_copy(0 if k < 2 else 1, 8, k).wait_send()
    z2_copy(0, 8).wait_send()
    for d in range(1, NY):
        y2_copy(0, 0, d).wait_send()
        y2_copy(0, 8, d).wait_send()

    @pl.loop(1, NZ)
    def _(d):
        zi_copy(d).wait_recv()

    t = zr[0].astype(F32)
    for k in range(1, NZ):
        t = t + zr[k].astype(F32)
    ig_ref[...] = jnp.concatenate([t[0:8], t[8:16]], axis=1).astype(BF16)
    save_ig.start()

    @pl.loop(1, NZ)
    def _(d):
        mz_copy(d).wait_recv()

    m_sum = mz[0].astype(F32)
    for k in range(1, NZ):
        m_sum = m_sum + mz[k].astype(F32)
    r_new = DECAY * rin_ref[...] + (1.0 - DECAY) * (unfold_lanes(m_sum, 0, 8) / FF + EPS)
    c_new = DECAY * cout_ref[...] + (1.0 - DECAY) * (unfold_lanes(m_sum, 8, 8) / FF + EPS)
    vec_ref[0:1, :] = r_new
    vec_ref[1:2, :] = c_new
    inv_r, inv_c = fold_lanes(1.0 / r_new, 8), fold_lanes(1.0 / c_new, 8)

    rp_in[...] = columns_of(r_new)
    rp_out[...] = columns_of(rout_new)

    @pl.loop(0, 8)
    def _(j):
        rows = pl.ds(pl.multiple_of(j * 128, 128), 128)
        r = rp_in[rows, :]
        for k in range(4):
            lanes = slice(k * 128, (k + 1) * 128)
            gin_ref[rows, lanes] = gin_ref[rows, lanes] * lax.rsqrt(r * vec_ref[2:3, lanes])
        rows = pl.ds(pl.multiple_of(j * 64, 64), 64)
        r = rp_out[rows, :]
        for k in range(8):
            lanes = slice(k * 128, (k + 1) * 128)
            gout_ref[rows, lanes] = gout_ref[rows, lanes] * lax.rsqrt(r * vec_ref[1:2, lanes])

    save_in.start()
    save_out.start()

    @pl.loop(1, NZ)
    def _(d):
        tz_copy(d).wait_recv()

    t = tz[0].astype(F32)
    for k in range(1, NZ):
        t = t + tz[k].astype(F32)
    n_in = jnp.sum(t[0:8] * inv_r, axis=0, keepdims=True)
    n_out = jnp.sum(t[8:16] * inv_c, axis=0, keepdims=True)
    which = lax.broadcasted_iota(jnp.int32, (8, 128), 0)
    nn[nar] = jnp.where(which < 4, n_in, n_out)
    for d in range(1, 8):
        nn_copy(d).start()
    @pl.loop(1, NZ)
    def _(d):
        mz_copy(d).wait_send()
        tz_copy(d).wait_send()
        zi_copy(d).wait_send()

    for d in range(1, 8):
        nn_copy(d).wait_recv()
    t = nn[0]
    for k in range(1, 8):
        t = t + nn[k]
    total = jnp.sum(t, axis=1, keepdims=True)
    inv = 1.0 / jnp.maximum(CLIP, jnp.sqrt(total / (float(D) * float(FF))))
    vec_ref[3:4, 0:512] = jnp.broadcast_to(inv[0:1], (1, 512))
    vec_ref[3:4, 512:1024] = jnp.broadcast_to(inv[4:5], (1, 512))
    save_vec.start()

    for d in range(1, 8):
        nn_copy(d).wait_send()
    for save in (save_in, save_out, save_ig, save_vec):
        save.wait()


ANY_SPEC = pl.BlockSpec(memory_space=pl.ANY)


def step(*args):
    dma = pltpu.SemaphoreType.DMA
    vmem = pltpu.VMEM
    shape = jax.ShapeDtypeStruct
    outs = (
        shape((8, 1024), BF16), shape((1024, 512), F32), shape((512, 1024), F32),
        shape((8, 1024), F32),
    )
    scratch = [
        vmem((8, 1024), BF16), vmem((8, 1024), BF16), vmem((1024, 512), BF16), vmem((512, 1024), BF16),
        vmem((1, 1024), F32), vmem((1, 512), F32), vmem((1, 512), F32), vmem((1, 1024), F32),
        vmem((8, 1024), BF16), vmem((1024, 512), F32), vmem((512, 1024), F32), vmem((8, 1024), F32),
        vmem((NZ, NY, 16, FIRST), BF16), vmem((NZ, NY, 16, 1024 - FIRST), BF16),
        vmem((512, 1024), BF16), vmem((512, 1024), BF16),
        vmem((512, 512), BF16), vmem((512, 512), BF16),
        vmem((8, 2, 32, 512), F32), vmem((8, 2, 32, 512), F32), vmem((8, 2, 32, 512), F32),
        vmem((8, NX, 16, 512), F32), vmem((8, NX, 16, 512), BF16), vmem((8, NX, 16, 512), BF16),
        vmem((NZ, NX, 16, 512), BF16),
        vmem((8, NY, 2, 16, 512), BF16), vmem((8, NY, 2, 16, 512), BF16),
        vmem((NZ, 16, 512), BF16), vmem((NZ, 16, 512), BF16),
        vmem((1024, 128), F32), vmem((512, 128), F32), vmem((1, 512), F32), vmem((1, 1024), F32),
        vmem((NY, 16, 128), F32), vmem((NZ, 16, 128), BF16),
        vmem((NY, 16, 128), F32), vmem((NZ, 16, 128), BF16),
        vmem((8, 8, 128), F32), vmem((8, 8, 128), F32),
        dma((8,)), dma((4,)),
        dma((NY,)), dma((NY,)), dma((2, 9, NY)), dma((2, 9, NY)),
        dma((2, 9, NY)), dma((2, 9, NY)), dma((2, 9)), dma((2, 9)), dma((8,)), dma((8,)),
        dma((8, NX)), dma((8, NX)), dma((8, 8)), dma((8, 8)),
        dma((8, NY)), dma((8, NY)), dma((NZ,)), dma((NZ,)),
        dma((NY,)), dma((NY,)), dma((NZ,)), dma((NZ,)),
        dma((NY,)), dma((NY,)), dma((NZ,)), dma((NZ,)),
        dma((8,)), dma((8,)), dma((8,)), dma((8,)),
    ]
    return pl.pallas_call(
        kernel,
        out_shape=outs,
        in_specs=[ANY_SPEC] * 8,
        out_specs=[ANY_SPEC] * 4,
        scratch_shapes=scratch,
        compiler_params=pltpu.CompilerParams(
            collective_id=1, has_side_effects=True, vmem_limit_bytes=56 * 2**20
        ),
        cost_estimate=pl.CostEstimate(
            flops=2700000000, bytes_accessed=8 * 2**20, transcendentals=100000
        ),
    )(*args)


STEPS = 2


def scale_kernel(
    ig_ref, gin_ref, gout_ref, vec_ref,
    ig_out, uin_ref, uout_ref, rin_out, cin_out, rout_out, cout_out,
):
    @pl.when(pl.program_id(0) == 0)
    def _():
        ig_out[...] = ig_ref[...]
        rin_out[...] = fold_lanes(vec_ref[0:1, :], 8)
        cout_out[...] = fold_lanes(vec_ref[1:2, :], 8)
        cin_out[...] = fold_lanes(vec_ref[2:3, 0:512], 4)
        rout_out[...] = fold_lanes(vec_ref[2:3, 512:1024], 4)

    inv_in = vec_ref[3:4, 0:512]
    inv_out = vec_ref[3:4, 512:1024]
    uin_ref[...] = (gin_ref[...] * inv_in).astype(BF16)
    for k in range(2):
        lanes = slice(k * 512, (k + 1) * 512)
        uout_ref[:, lanes] = (gout_ref[:, lanes] * inv_out).astype(BF16)


def scale(*args):
    shape = jax.ShapeDtypeStruct
    whole = lambda *dims: pl.BlockSpec(dims, lambda j: (0, 0))
    big = lambda *dims: pl.BlockSpec(dims, lambda j: (j, 0))
    return pl.pallas_call(
        scale_kernel,
        grid=(STEPS,),
        in_specs=[
            whole(8, 1024), big(1024 // STEPS, 512), big(512 // STEPS, 1024), whole(8, 1024),
        ],
        out_specs=[
            whole(8, 1024), big(1024 // STEPS, 512), big(512 // STEPS, 1024),
            whole(8, 128), whole(4, 128), whole(4, 128), whole(8, 128),
        ],
        out_shape=(
            shape((8, 1024), BF16), shape((1024, 512), BF16), shape((512, 1024), BF16),
            shape((8, 128), F32), shape((4, 128), F32), shape((4, 128), F32), shape((8, 128), F32),
        ),
        compiler_params=pltpu.CompilerParams(vmem_limit_bytes=56 * 2**20),
    )(*args)


def per_device(inputs, out_grad, w_in, w_out, row_in, col_in, row_out, col_out):
    line = lambda v: v.reshape(1, -1)
    whole = step(
        inputs, out_grad, w_in, w_out, line(row_in), line(col_in), line(row_out), line(col_out)
    )
    ig, update_in, update_out, rin, cin, rout, cout = scale(*whole)
    return (
        ig, update_in, update_out,
        rin.reshape(-1), cin.reshape(-1), rout.reshape(-1), cout.reshape(-1),
    )


def solution(mesh):
    placed = (
        P("mp", "narrow"),
        P("mp", "narrow"),
        P("narrow", "mp"),
        P("mp", "narrow"),
        P("narrow"),
        P("mp"),
        P("mp"),
        P("narrow"),
    )
    return jax.shard_map(
        per_device,
        mesh=mesh,
        in_specs=placed,
        out_specs=(
            P("mp", "narrow"),
            P("narrow", "mp"),
            P("mp", "narrow"),
            P("narrow"),
            P("mp"),
            P("mp"),
            P("narrow"),
        ),
        check_vma=False,
    )
```

```python
import functools

import jax
import jax.numpy as jnp
from jax import lax
from jax.experimental import pallas as pl
from jax.experimental.pallas import tpu as pltpu
from jax.sharding import PartitionSpec as P

D = 8192
FF = 32768
DECAY = 0.8
EPS = 1e-06
CLIP = 0.01

NY, NZ, NX = 4, 16, 4
F32, BF16 = jnp.float32, jnp.bfloat16
MESH = pl.DeviceIdType.MESH
EXACT = lax.Precision.HIGHEST
LAG = (1, 3, 5, 7)
FIRST = 256
FAR_FIRST = (8, 7, 9, 6, 10, 5, 11, 4, 12, 3, 13, 2, 14, 1, 15)


def dot(a, b, dims, precision=None):
    return lax.dot_general(
        a, b, ((dims[0], dims[1]), ((), ())), precision=precision, preferred_element_type=F32
    )


def fold_lanes(row, parts):
    return jnp.concatenate([row[:, k * 128 : (k + 1) * 128] for k in range(parts)], axis=0)


def unfold_lanes(block, start, parts):
    return jnp.concatenate([block[start + k : start + k + 1, :] for k in range(parts)], axis=1)


def lane_fold(q):
    out = q[:, 0:128]
    for k in range(1, q.shape[1] // 128):
        out = out + q[:, k * 128 : (k + 1) * 128]
    return out


def columns_of(row):
    return jnp.transpose(jnp.broadcast_to(row, (128, row.shape[1])))


def kernel(
    x_hbm, dy_hbm, win_hbm, wout_hbm, rin_hbm, cin_hbm, rout_hbm, cout_hbm,
    ig_ref, gin_ref, gout_ref, vec_ref,
    x_ref, dy_ref, win_ref, wout_ref, rin_ref, cin_ref, rout_ref, cout_ref,
    g1, g2, xs, ds, acts, hgs, keep, give, cx, tot, sx, xr, hh,
    ys, yr, zs, zr,
    rp_in, rp_out, cs_in, cs_out,
    my, mz, ty, tz, nb, nn,
    w_sem,
    yg_s, yg_r, zg_s, zg_r, y2_s, y2_r, z2_s, z2_r, cx_s, cx_r, xr_s, xr_r, xg_s, xg_r,
    yi_s, yi_r, zi_s, zi_r, my_s, my_r, mz_s, mz_r, ty_s, ty_r, tz_s, tz_r,
    nb_s, nb_r, nn_s, nn_r,
):
    mp = lax.axis_index("mp")
    nar = lax.axis_index("narrow")
    y, z = mp // NZ, lax.rem(mp, NZ)
    x, c = nar // 2, lax.rem(nar, 2)

    def at_y(d):
        return (lax.rem(y + d, NY) * NZ + z, nar)

    def at_z(d):
        return (y * NZ + lax.rem(z + d, NZ), nar)

    def at_x(d):
        return (mp, lax.rem(x + d, NX) * 2 + c)

    def at_n(d):
        return (mp, lax.rem(nar + d, 8))

    other = (mp, x * 2 + 1 - c)

    def remote(src, dst, ssem, rsem, dev):
        return pltpu.make_async_remote_copy(
            src_ref=src, dst_ref=dst, send_sem=ssem, recv_sem=rsem,
            device_id=dev, device_id_type=MESH,
        )

    barrier = pltpu.get_barrier_semaphore()
    greet = [at_y(1), at_y(2), at_y(3), at_z(1), at_z(NZ - 1), at_z(2), at_z(NZ - 2), at_x(1), at_x(2), at_x(3), other]
    for dev in greet:
        pl.semaphore_signal(barrier, inc=1, device_id=dev, device_id_type=MESH)

    loads = [
        pltpu.make_async_copy(src, dst, w_sem.at[k])
        for k, (src, dst) in enumerate((
            (x_hbm, x_ref), (dy_hbm, dy_ref), (win_hbm, win_ref), (wout_hbm, wout_ref),
            (rin_hbm, rin_ref), (cin_hbm, cin_ref), (rout_hbm, rout_ref), (cout_hbm, cout_ref),
        ))
    ]
    for load in loads:
        load.start()
    loads[0].wait()
    loads[1].wait()
    mine = jnp.concatenate([x_ref[...].astype(F32), dy_ref[...].astype(F32)], axis=0).astype(BF16)
    g1[z, y] = mine[:, 0:FIRST]
    g2[z, y] = mine[:, FIRST:1024]
    vec_ref[...] = jnp.zeros_like(vec_ref)
    pl.semaphore_wait(barrier, len(greet))

    def y_copy(d):
        return remote(g1.at[z, y], g1.at[z, y], yg_s.at[d], yg_r.at[d], at_y(d))

    def z_way(way, r):
        hop = jnp.where(r > 1, 2, 1)
        back = r - hop
        row = lax.rem(z + (NZ - back if way == 0 else back), NZ)
        return row, at_z(hop if way == 0 else NZ - hop)

    def z_copy(way, r, k):
        row, dev = z_way(way, r)
        ref = g1.at[row, lax.rem(y + NY - k, NY)]
        return remote(ref, ref, zg_s.at[way, r, k], zg_r.at[way, r, k], dev)

    def z2_copy(way, r):
        row, dev = z_way(way, r)
        ref = g2.at[row, y]
        return remote(ref, ref, z2_s.at[way, r], z2_r.at[way, r], dev)

    def y2_copy(way, s, d):
        row = lax.rem(z + (NZ - s if way == 0 else s), NZ)
        ref = g2.at[row, y]
        return remote(ref, ref, y2_s.at[way, s, d], y2_r.at[way, s, d], at_y(d))

    def pair(s):
        first = lax.rem(z + NZ - s, NZ)
        second = lax.rem(z + lax.rem(s, 8), NZ)
        return jnp.where(c == 0, first, second), jnp.where(c == 0, second, first)

    def rows32(cell):
        return pl.ds(pl.multiple_of(cell * 32, 32), 32)

    def split16(block, width):
        block = block.astype(F32)
        return (
            block[:, 0:8, :].reshape(32, width).astype(BF16),
            block[:, 8:16, :].reshape(32, width).astype(BF16),
        )

    def cx_copy(s):
        i = s - 1
        return remote(give.at[i], cx.at[i], cx_s.at[i], cx_r.at[i], other)

    def xr_copy(s, d):
        i = s - 1
        to = lax.rem(x + d, NX)
        return remote(sx.at[i, to], xr.at[i, x], xr_s.at[i, d], xr_r.at[i, d], at_x(d))

    def xg_copy(s, k):
        d, flip = k // 2, k % 2
        ref = hh.at[pair(s)[0], x]
        core = 1 - c if flip else c
        dev = (mp, lax.rem(x + d, NX) * 2 + core)
        return remote(ref, ref, xg_s.at[s - 1, k], xg_r.at[s - 1, k], dev)

    def yi_copy(s, d):
        i = s - 1
        to = lax.rem(y + d, NY)
        return remote(ys.at[i, to], yr.at[i, y], yi_s.at[i, d], yi_r.at[i, d], at_y(d))

    def zi_copy(d):
        to = lax.rem(z + d, NZ)
        return remote(zs.at[to], zr.at[z], zi_s.at[d], zi_r.at[d], at_z(d))

    def project(s):
        cells = pair(s)
        got = []
        for cell in cells:
            low, high = split16(g1[cell], FIRST), split16(g2[cell], 1024 - FIRST)
            got.append([jnp.concatenate([a, b], axis=1) for a, b in zip(low, high)])
        xb = jnp.concatenate([g[0] for g in got], axis=0)
        db = jnp.concatenate([g[1] for g in got], axis=0)
        pre = dot(xb, win_ref[...], ((1,), (0,)))
        up = dot(db, wout_ref[...], ((1,), (1,)))
        i = s - 1
        keep[i, 0] = pre[0:32]
        keep[i, 1] = up[0:32]
        give[i, 0] = pre[32:64]
        give[i, 1] = up[32:64]
        cx_copy(s).start()
        for g, cell in zip(got, cells):
            xs[rows32(cell), :] = g[0]
            ds[rows32(cell), :] = g[1]

    def spread(s):
        i = s - 1
        cx_copy(s).wait_recv()
        t = keep[i] + cx[i]
        t = jnp.concatenate([t[0].reshape(4, 8, 512), t[1].reshape(4, 8, 512)], axis=1)
        tot[i] = t
        sx[i] = t.astype(BF16)
        for d in (2, 1, 3):
            xr_copy(s, d).start()

    def activate(s):
        i = s - 1
        t = tot[i, x]
        for d in (1, 3, 2):
            xr_copy(s, d).wait_recv()
            t = t + xr[i, lax.rem(x + NX - d, NX)].astype(F32)
        pre, up = t[0:8], t[8:16]
        sig = 1.0 / (1.0 + jnp.exp(-pre))
        hh[pair(s)[0], x] = jnp.concatenate(
            [pre * sig, up * (sig * (1.0 + pre * (1.0 - sig)))], axis=0
        ).astype(BF16)
        for k in (4, 5, 2, 6, 3, 7, 1):
            xg_copy(s, k).start()

    def back_project(s):
        for k in range(1, 8):
            xg_copy(s, k).wait_recv()
        cells = pair(s)
        got = [split16(hh[cell], 512) for cell in cells]
        p = dot(jnp.concatenate([g[1] for g in got], axis=0), win_ref[...], ((1,), (1,)))
        p = p.reshape(2, 4, 8, 1024)
        p = jnp.concatenate([p[..., 0:512], p[..., 512:1024]], axis=2).astype(BF16)
        for k in range(NY):
            ys[s - 1, k] = p[:, k]
        for d in (2, 1, 3):
            yi_copy(s, d).start()
        for g, cell in zip(got, cells):
            acts[rows32(cell), :] = g[0]
            hgs[rows32(cell), :] = g[1]

    def deliver(s):
        i = s - 1
        yr[i, y] = ys[i, y]
        for d in (1, 3, 2):
            yi_copy(s, d).wait_recv()
        t = (yr[i, 0].astype(F32) + yr[i, 1].astype(F32)) + (
            yr[i, 2].astype(F32) + yr[i, 3].astype(F32)
        )
        for k, cell in enumerate(pair(s)):
            zs[cell] = t[k].astype(BF16)

        zi_copy(NZ - s).start()

        @pl.when(s < 8)
        def _():
            zi_copy(lax.rem(s, NZ)).start()

    for d in (2, 1, 3):
        y_copy(d).start()
    for r in (2, 1):
        for way in range(2):
            z2_copy(way, r).start()
            z_copy(way, r, 0).start()
    for k in (1, 3, 2):
        y_copy(k).wait_recv()
        for r in (2, 1):
            for way in range(2):
                z_copy(way, r, k).start()
    for r in (1, 2):
        for way in range(2):
            z2_copy(way, r).wait_recv()
            z2_copy(way, r + 2).start()
            for d in (2, 1, 3):
                y2_copy(way, r, d).start()
    for d in (2, 1, 3):
        y2_copy(0, 0, d).start()
    for load in loads[2:]:
        load.wait()

    @pl.loop(1, 8 + LAG[2] + 1)
    def _(s):
        @pl.when(s < 6)
        def _():
            for k in (0, 1, 3, 2):
                for way in range(2):
                    z_copy(way, s, k).wait_recv()
                    z_copy(way, s + 2, k).start()
            for way in range(2):
                z2_copy(way, s + 2).wait_recv()
                if way == 0:

                    @pl.when(s < 5)
                    def _():
                        z2_copy(0, s + 4).start()
                else:

                    @pl.when(s < 4)
                    def _():
                        z2_copy(1, s + 4).start()

                for d in (2, 1, 3):
                    y2_copy(way, s + 2, d).start()

        @pl.when(s == 6)
        def _():
            for k in (0, 1, 3, 2):
                for way in range(2):
                    z_copy(way, 6, k).wait_recv()
                    if (k < 2) == (way == 0):
                        z_copy(way, 8, k).start()
            z2_copy(0, 8).wait_recv()
            for d in (2, 1, 3):
                y2_copy(0, 8, d).start()

        @pl.when(s == 7)
        def _():
            for k in (0, 1, 3, 2):
                for way in range(2):
                    z_copy(way, 7, k).wait_recv()

        @pl.when(s < 8)
        def _():
            for way in range(2):
                for d in (1, 3, 2):
                    y2_copy(way, s, d).wait_recv()

        @pl.when(s == 8)
        def _():
            for k in (0, 1, 3, 2):
                z_copy(0 if k < 2 else 1, 8, k).wait_recv()
            for d in (1, 3, 2):
                y2_copy(0, 0, d).wait_recv()
                y2_copy(0, 8, d).wait_recv()

        def stage(lag, run):
            @pl.when(jnp.logical_and(s > lag, s <= 8 + lag))
            def _():
                run(s - lag)

        stage(LAG[0], spread)
        stage(LAG[1], activate)

        @pl.when(s <= 8)
        def _():
            project(s)

        stage(LAG[2], back_project)
        stage(LAG[3], deliver)

    rp_out[...] = jnp.zeros_like(rp_out)
    cs_in[...] = jnp.zeros_like(cs_in)

    @pl.loop(0, 4)
    def _(j):
        cols = pl.ds(pl.multiple_of(j * 256, 256), 256)
        g = dot(acts[...], ds[:, cols], ((0,), (0,)))
        gout_ref[:, cols] = g
        q = g * g
        cs_out[:, cols] = jnp.sum(q, axis=0, keepdims=True)
        rp_out[...] += lane_fold(q)
        g = dot(xs[:, cols], hgs[...], ((0,), (0,)))
        gin_ref[cols, :] = g
        q = g * g
        cs_in[...] += jnp.sum(q, axis=0, keepdims=True)
        rp_in[cols, :] = lane_fold(q)

    ones = jnp.ones((8, 128), F32)

    def my_copy(d):
        return remote(my.at[y], my.at[y], my_s.at[d], my_r.at[d], at_y(d))

    def mz_copy(d):
        return remote(mz.at[z], mz.at[z], mz_s.at[d], mz_r.at[d], at_z(d))

    def ty_copy(d):
        return remote(ty.at[y], ty.at[y], ty_s.at[d], ty_r.at[d], at_y(d))

    def tz_copy(d):
        return remote(tz.at[z], tz.at[z], tz_s.at[d], tz_r.at[d], at_z(d))

    def nb_copy(d):
        return remote(nb.at[nar], nb.at[nar], nb_s.at[d], nb_r.at[d], at_n(d))

    def nn_copy(d):
        return remote(nn.at[nar], nn.at[nar], nn_s.at[d], nn_r.at[d], at_n(d))

    row_sums_out = dot(ones, rp_out[...], ((1,), (1,)), EXACT)[0:1]
    nb[nar] = jnp.concatenate([fold_lanes(cs_in[...], 4), fold_lanes(row_sums_out, 4)], axis=0)
    for d in range(1, 8):
        nb_copy(d).start()
    row_sums_in = dot(ones, rp_in[...], ((1,), (1,)), EXACT)[0:1]
    my[y] = jnp.concatenate([fold_lanes(row_sums_in, 8), fold_lanes(cs_out[...], 8)], axis=0)
    for d in range(1, NY):
        my_copy(d).start()

    for s in range(8 + LAG[2] - LAG[3] + 1, 9):
        deliver(s)
    zr[z] = zs[z]

    for d in range(1, 8):
        nb_copy(d).wait_recv()
    n_sum = nb[0]
    for k in range(1, 8):
        n_sum = n_sum + nb[k]
    cin_new = DECAY * cin_ref[...] + (1.0 - DECAY) * (unfold_lanes(n_sum, 0, 4) / D + EPS)
    rout_new = DECAY * rout_ref[...] + (1.0 - DECAY) * (unfold_lanes(n_sum, 4, 4) / D + EPS)
    vec_ref[2:3, 0:512] = cin_new
    vec_ref[2:3, 512:1024] = rout_new

    inv_cin = 1.0 / cin_new
    rp_out[...] = columns_of(1.0 / rout_new)

    @pl.loop(0, 4)
    def _(j):
        cols = pl.ds(pl.multiple_of(j * 256, 256), 256)
        g = gout_ref[:, cols]
        q = g * g
        w = rp_out[...]
        q = jnp.concatenate([q[:, 0:128] * w, q[:, 128:256] * w], axis=1)
        cs_out[:, cols] = jnp.sum(q, axis=0, keepdims=True)
        g = gin_ref[cols, :]
        rp_in[cols, :] = lane_fold(g * g * inv_cin)

    t_in = dot(ones, rp_in[...], ((1,), (1,)), EXACT)[0:1]
    ty[y] = jnp.concatenate([fold_lanes(t_in, 8), fold_lanes(cs_out[...], 8)], axis=0)
    for d in range(1, NY):
        ty_copy(d).start()

    for d in range(1, NY):
        my_copy(d).wait_recv()
    mz[z] = ((my[0] + my[1]) + (my[2] + my[3])).astype(BF16)

    for d in FAR_FIRST:
        mz_copy(d).start()

    for d in range(1, NY):
        ty_copy(d).wait_recv()
    tz[z] = ((ty[0] + ty[1]) + (ty[2] + ty[3])).astype(BF16)

    for d in FAR_FIRST:
        tz_copy(d).start()

    for d in range(1, NY):
        y_copy(d).wait_send()
        my_copy(d).wait_send()
        ty_copy(d).wait_send()

    @pl.loop(1, 9)
    def _(s):
        cx_copy(s).wait_send()
        for k in range(1, 8):
            xg_copy(s, k).wait_send()
        for d in range(1, NX):
            xr_copy(s, d).wait_send()
            yi_copy(s, d).wait_send()

    for d in range(1, 8):
        nb_copy(d).wait_send()

    @pl.loop(1, 8)
    def _(s):
        for way in range(2):
            z2_copy(way, s).wait_send()
            for k in range(NY):
                z_copy(way, s, k).wait_send()
            for d in range(1, NY):
                y2_copy(way, s, d).wait_send()

    for k in range(NY):
        z_copy(0 if k < 2 else 1, 8, k).wait_send()
    z2_copy(0, 8).wait_send()
    for d in range(1, NY):
        y2_copy(0, 0, d).wait_send()
        y2_copy(0, 8, d).wait_send()

    @pl.loop(1, NZ)
    def _(d):
        zi_copy(d).wait_recv()

    t = zr[0].astype(F32)
    for k in range(1, NZ):
        t = t + zr[k].astype(F32)
    ig_ref[...] = jnp.concatenate([t[0:8], t[8:16]], axis=1).astype(BF16)

    @pl.loop(1, NZ)
    def _(d):
        mz_copy(d).wait_recv()

    m_sum = mz[0].astype(F32)
    for k in range(1, NZ):
        m_sum = m_sum + mz[k].astype(F32)
    r_new = DECAY * rin_ref[...] + (1.0 - DECAY) * (unfold_lanes(m_sum, 0, 8) / FF + EPS)
    c_new = DECAY * cout_ref[...] + (1.0 - DECAY) * (unfold_lanes(m_sum, 8, 8) / FF + EPS)
    vec_ref[0:1, :] = r_new
    vec_ref[1:2, :] = c_new
    inv_r, inv_c = fold_lanes(1.0 / r_new, 8), fold_lanes(1.0 / c_new, 8)

    rp_in[...] = columns_of(r_new)
    rp_out[...] = columns_of(rout_new)

    @pl.loop(0, 8)
    def _(j):
        rows = pl.ds(pl.multiple_of(j * 128, 128), 128)
        r = rp_in[rows, :]
        for k in range(4):
            lanes = slice(k * 128, (k + 1) * 128)
            gin_ref[rows, lanes] = gin_ref[rows, lanes] * lax.rsqrt(r * vec_ref[2:3, lanes])
        rows = pl.ds(pl.multiple_of(j * 64, 64), 64)
        r = rp_out[rows, :]
        for k in range(8):
            lanes = slice(k * 128, (k + 1) * 128)
            gout_ref[rows, lanes] = gout_ref[rows, lanes] * lax.rsqrt(r * vec_ref[1:2, lanes])

    @pl.loop(1, NZ)
    def _(d):
        tz_copy(d).wait_recv()

    t = tz[0].astype(F32)
    for k in range(1, NZ):
        t = t + tz[k].astype(F32)
    n_in = jnp.sum(t[0:8] * inv_r, axis=0, keepdims=True)
    n_out = jnp.sum(t[8:16] * inv_c, axis=0, keepdims=True)
    which = lax.broadcasted_iota(jnp.int32, (8, 128), 0)
    nn[nar] = jnp.where(which < 4, n_in, n_out)
    for d in range(1, 8):
        nn_copy(d).start()
    @pl.loop(1, NZ)
    def _(d):
        mz_copy(d).wait_send()
        tz_copy(d).wait_send()
        zi_copy(d).wait_send()

    for d in range(1, 8):
        nn_copy(d).wait_recv()
    t = nn[0]
    for k in range(1, 8):
        t = t + nn[k]
    total = jnp.sum(t, axis=1, keepdims=True)
    inv = 1.0 / jnp.maximum(CLIP, jnp.sqrt(total / (float(D) * float(FF))))
    vec_ref[3:4, 0:512] = jnp.broadcast_to(inv[0:1], (1, 512))
    vec_ref[3:4, 512:1024] = jnp.broadcast_to(inv[4:5], (1, 512))

    for d in range(1, 8):
        nn_copy(d).wait_send()


VMEM_SPEC = pl.BlockSpec(memory_space=pltpu.VMEM)
ANY_SPEC = pl.BlockSpec(memory_space=pl.ANY)


def step(*args):
    dma = pltpu.SemaphoreType.DMA
    vmem = pltpu.VMEM
    shape = jax.ShapeDtypeStruct
    outs = (
        vmem((8, 1024), BF16), vmem((1024, 512), F32), vmem((512, 1024), F32),
        vmem((8, 1024), F32),
    )
    scratch = [
        vmem((8, 1024), BF16), vmem((8, 1024), BF16), vmem((1024, 512), BF16), vmem((512, 1024), BF16),
        vmem((1, 1024), F32), vmem((1, 512), F32), vmem((1, 512), F32), vmem((1, 1024), F32),
        vmem((NZ, NY, 16, FIRST), BF16), vmem((NZ, NY, 16, 1024 - FIRST), BF16),
        vmem((512, 1024), BF16), vmem((512, 1024), BF16),
        vmem((512, 512), BF16), vmem((512, 512), BF16),
        vmem((8, 2, 32, 512), F32), vmem((8, 2, 32, 512), F32), vmem((8, 2, 32, 512), F32),
        vmem((8, NX, 16, 512), F32), vmem((8, NX, 16, 512), BF16), vmem((8, NX, 16, 512), BF16),
        vmem((NZ, NX, 16, 512), BF16),
        vmem((8, NY, 2, 16, 512), BF16), vmem((8, NY, 2, 16, 512), BF16),
        vmem((NZ, 16, 512), BF16), vmem((NZ, 16, 512), BF16),
        vmem((1024, 128), F32), vmem((512, 128), F32), vmem((1, 512), F32), vmem((1, 1024), F32),
        vmem((NY, 16, 128), F32), vmem((NZ, 16, 128), BF16),
        vmem((NY, 16, 128), F32), vmem((NZ, 16, 128), BF16),
        vmem((8, 8, 128), F32), vmem((8, 8, 128), F32),
        dma((8,)),
        dma((NY,)), dma((NY,)), dma((2, 9, NY)), dma((2, 9, NY)),
        dma((2, 9, NY)), dma((2, 9, NY)), dma((2, 9)), dma((2, 9)), dma((8,)), dma((8,)),
        dma((8, NX)), dma((8, NX)), dma((8, 8)), dma((8, 8)),
        dma((8, NY)), dma((8, NY)), dma((NZ,)), dma((NZ,)),
        dma((NY,)), dma((NY,)), dma((NZ,)), dma((NZ,)),
        dma((NY,)), dma((NY,)), dma((NZ,)), dma((NZ,)),
        dma((8,)), dma((8,)), dma((8,)), dma((8,)),
    ]
    return pl.pallas_call(
        kernel,
        out_shape=outs,
        in_specs=[pl.BlockSpec(memory_space=pltpu.HBM)] * 8,
        out_specs=[VMEM_SPEC] * 4,
        scratch_shapes=scratch,
        compiler_params=pltpu.CompilerParams(
            collective_id=1, has_side_effects=True, vmem_limit_bytes=52 * 2**20
        ),
        cost_estimate=pl.CostEstimate(
            flops=2700000000, bytes_accessed=8 * 2**20, transcendentals=100000
        ),
    )(*args)


STEPS = 2


def scale_kernel(
    ig_ref, gin_ref, gout_ref, vec_ref,
    ig_out, uin_ref, uout_ref, rin_out, cin_out, rout_out, cout_out,
):
    @pl.when(pl.program_id(0) == 0)
    def _():
        ig_out[...] = ig_ref[...]
        rin_out[...] = fold_lanes(vec_ref[0:1, :], 8)
        cout_out[...] = fold_lanes(vec_ref[1:2, :], 8)
        cin_out[...] = fold_lanes(vec_ref[2:3, 0:512], 4)
        rout_out[...] = fold_lanes(vec_ref[2:3, 512:1024], 4)

    inv_in = vec_ref[3:4, 0:512]
    inv_out = vec_ref[3:4, 512:1024]
    many, few = 1024 // STEPS, 512 // STEPS
    step_id = pl.program_id(0)
    rows = pl.ds(pl.multiple_of(step_id * many, many), many)
    uin_ref[...] = (gin_ref[rows, :] * inv_in).astype(BF16)
    rows = pl.ds(pl.multiple_of(step_id * few, few), few)
    for k in range(2):
        lanes = slice(k * 512, (k + 1) * 512)
        uout_ref[:, lanes] = (gout_ref[rows, lanes] * inv_out).astype(BF16)


def scale(*args):
    shape = jax.ShapeDtypeStruct
    whole = lambda *dims: pl.BlockSpec(dims, lambda j: (0, 0))
    big = lambda *dims: pl.BlockSpec(dims, lambda j: (j, 0))
    return pl.pallas_call(
        scale_kernel,
        grid=(STEPS,),
        in_specs=[
            VMEM_SPEC, VMEM_SPEC, VMEM_SPEC, VMEM_SPEC,
        ],
        out_specs=[
            whole(8, 1024), big(1024 // STEPS, 512), big(512 // STEPS, 1024),
            whole(8, 128), whole(4, 128), whole(4, 128), whole(8, 128),
        ],
        out_shape=(
            shape((8, 1024), BF16), shape((1024, 512), BF16), shape((512, 1024), BF16),
            shape((8, 128), F32), shape((4, 128), F32), shape((4, 128), F32), shape((8, 128), F32),
        ),
        compiler_params=pltpu.CompilerParams(vmem_limit_bytes=48 * 2**20),
    )(*args)


def per_device(inputs, out_grad, w_in, w_out, row_in, col_in, row_out, col_out):
    line = lambda v: v.reshape(1, -1)
    whole = step(
        inputs, out_grad, w_in, w_out, line(row_in), line(col_in), line(row_out), line(col_out)
    )
    ig, update_in, update_out, rin, cin, rout, cout = scale(*whole)
    return (
        ig, update_in, update_out,
        rin.reshape(-1), cin.reshape(-1), rout.reshape(-1), cout.reshape(-1),
    )


def solution(mesh):
    placed = (
        P("mp", "narrow"),
        P("mp", "narrow"),
        P("narrow", "mp"),
        P("mp", "narrow"),
        P("narrow"),
        P("mp"),
        P("mp"),
        P("narrow"),
    )
    return jax.shard_map(
        per_device,
        mesh=mesh,
        in_specs=placed,
        out_specs=(
            P("mp", "narrow"),
            P("narrow", "mp"),
            P("mp", "narrow"),
            P("narrow"),
            P("mp"),
            P("mp"),
            P("narrow"),
        ),
        check_vma=False,
    )
```
